256 devices in a mesh: replica: 16 (over y_lo, z), fsdp: 16 (over y_hi, x, core).
Axes of the slice: x: 4, y: 4 (y_hi: 2, y_lo: 2; y = y_hi * 2 + y_lo), z: 8, core: 2. Of those that a mesh axis runs over, the one named last changes fastest.
Arguments:
- inputs: bfloat16 [98304, 4096], P(('replica', 'fsdp')), may hold values from -24 to 24
- projection: bfloat16 [16, 4096, 1024], P('replica', 'fsdp'), may hold values from -0.09375 to 0.09375
- cotangent: bfloat16 [98304, 1024], P(('replica', 'fsdp')), may hold values from -0.07470703 to 0.07470703
- pseudo_grad: bfloat16 [16, 2048, 4096], P('replica', 'fsdp'), may hold values from -6 to 6
- outer_params: float32 [2048, 4096], P('fsdp', 'replica'), may hold values from -0.125 to 0.125
- outer_momentum: float32 [2048, 4096], P('fsdp', 'replica'), may hold values from -1.5 to 1.5
Outputs:
- keys_values: bfloat16 [98304, 1024], P(('replica', 'fsdp'))
- proj_grad: float32 [16, 4096, 1024], P('replica', 'fsdp')
- new_params: float32 [2048, 4096], P('fsdp', 'replica')
- new_momentum: float32 [2048, 4096], P('fsdp', 'replica')
- local_weights: bfloat16 [2048, 4096], P('fsdp')
The draws below stay inside these ranges and needn't reach their ends.
All inputs are finite; a program needn't handle non-finite values.
Results may differ from the reference program's by a relative error of at most 0.0029.
Values may be sent and summed in bfloat16 or wider, within the bound.
A program may use at most 128 MiB of HBM per device.

```python
import jax
import jax.numpy as jnp
from jax import lax

D = 4096
TOK_DEV = 384
REPLICAS = 16
TOKENS = 98304
KV_COLS = 1024
FRAG_ROWS = 2048
N_FSDP = 16


def strengthened(drawn, own_key, source, target, shards_of, factor):
    def block_of(axis_at):
        return (jnp.arange(drawn.shape[axis_at]) // (drawn.shape[axis_at] // shards_of)).reshape((-1,) + (1,) * (drawn.ndim - 1 - axis_at))

    near = jax.random.permutation(own_key, shards_of)[block_of(target)]
    other_side = (block_of(target) + shards_of // 2) % shards_of
    return jnp.where((block_of(source) == near) | (block_of(source) == other_side), factor * drawn, drawn)


def levels(stream_key, dims, pieces, low, largest):
    def one(axis_at, parts):
        steps = jax.random.uniform(jax.random.fold_in(jax.random.fold_in(stream_key, 6), axis_at), (parts,), jnp.float32, low / len(pieces), largest / len(pieces))
        return jnp.repeat(jnp.exp(steps), dims[axis_at] // parts).reshape((-1,) + (1,) * (len(dims) - axis_at - 1))

    gain = one(*pieces[0])
    for cut in pieces[1:]:
        gain = gain * one(*cut)
    return gain


def normal_values(rng, extent, width, most, split=(), dtype=jnp.bfloat16):
    gain = levels(rng, extent, split, -0.22, 0.18) if split else 1.0
    entries = jax.random.normal(rng, extent, jnp.float32) * width * gain
    return jnp.minimum(jnp.maximum(entries, -most), most).astype(dtype)


def heavy_noise(own_key, extent, spread, reach, shards, heavy, kind=jnp.bfloat16):
    result = spread * jax.random.normal(own_key, extent, jnp.float32)
    if shards:
        result = result * levels(own_key, extent, shards, -0.22, 0.18)
    return jnp.clip(strengthened(result, jax.random.fold_in(own_key, 3), *heavy), -reach, reach).astype(kind)


def setup_inputs(seed: int = 0) -> dict:
    splits = jax.random.split(jax.random.key(seed), 7)
    inputs = heavy_noise(splits[0], (TOKENS, D), 1.0, 24.0, ((0, 256),), (0, 1, 256, 6.0))
    projection = normal_values(splits[1], (REPLICAS, D, KV_COLS), D ** -0.5, 0.09375, ((0, 16), (1, 16)))
    cotangent = normal_values(splits[2], (TOKENS, KV_COLS), 0.0125, 0.07470703, ((0, 256),))
    pseudo_grad = heavy_noise(splits[3], (REPLICAS, FRAG_ROWS, D), 1.0, 6.0, ((0, 16), (1, 16)), (0, 2, 16, 2.0))
    outer_params = normal_values(splits[4], (FRAG_ROWS, D), FRAG_ROWS ** -0.5, 0.125, ((0, 16), (1, 16)), jnp.float32)
    outer_momentum = normal_values(splits[5], (FRAG_ROWS, D), 0.25, 1.5, ((0, 16), (1, 16)), jnp.float32)
    return {"inputs": inputs, "projection": projection, "cotangent": cotangent, "pseudo_grad": pseudo_grad, "outer_params": outer_params, "outer_momentum": outer_momentum}


outer_rate = 0.7
outer_beta = 0.9


def reference(inputs, projection, cotangent, pseudo_grad, outer_params, outer_momentum):
    replica_tokens = TOK_DEV * N_FSDP
    grouped = inputs.reshape(REPLICAS, replica_tokens, D)
    upstream = cotangent.reshape(REPLICAS, replica_tokens, KV_COLS)

    def one_replica(operands):
        tokens_in, weight, incoming = operands
        outputs = jnp.dot(tokens_in, weight, preferred_element_type=jnp.float32).astype(jnp.bfloat16)
        token_blocks = tokens_in.reshape(N_FSDP, TOK_DEV, D)
        grad_blocks = incoming.reshape(N_FSDP, TOK_DEV, KV_COLS)

        def add_block(running, block_pair):
            partial_term = jnp.dot(block_pair[0].T, block_pair[1], preferred_element_type=jnp.float32)
            rounded = lax.optimization_barrier(partial_term.astype(jnp.bfloat16)).astype(jnp.float32)
            return running + rounded, None

        gradient, unused = lax.scan(add_block, jnp.zeros((D, KV_COLS), jnp.float32), (token_blocks, grad_blocks))
        return outputs, gradient

    outputs, gradient = lax.map(one_replica, (grouped, projection, upstream))
    keys_values = outputs.reshape(TOKENS, KV_COLS)
    average = jnp.sum(pseudo_grad.astype(jnp.float32), axis=0) / REPLICAS
    moment = outer_beta * outer_momentum + average
    params = outer_params - outer_rate * (outer_beta * moment + average)
    return keys_values, gradient, params, moment, params.astype(jnp.bfloat16)
```

```python
import jax
import jax.numpy as jnp
from jax import lax
from jax.experimental import pallas as pl
from jax.experimental.pallas import tpu as pltpu
from jax.sharding import PartitionSpec as P

outer_rate = 0.7
outer_beta = 0.9

MESH = pl.DeviceIdType.MESH
bf16 = jnp.bfloat16
f32 = jnp.float32

TOK = 384
D = 4096
HALF = 2048
KV = 1024
ROWS = 256
CUT = 160
MID1 = CUT // 2
MID2 = CUT + (ROWS - CUT) // 2
FR = 128
FC = 256

MESSAGES = (
    ["yP1", "yP2_0", "yP2_1", "yP2_3", "yP2_2a", "yP2_2b"]
    + [d + k for d in ("xp", "xm") for k in ("P2", "P1", "Q1", "fP2", "fP1", "fQ1")]
    + ["xs%d" % r for r in range(8)]
    + ["cs", "kv0", "kv1"]
    + ["b%s%d" % (d, y) for d in "pm" for y in (0, 1)]
    + ["c%s%d%s" % (d, y, h) for d in "pm" for y in (0, 1) for h in "ab"]
    + ["d%d" % x for x in range(4)]
    + ["e", "gp", "gm", "hp", "hm"]
    + ["z%s%d" % (d, k) for d in "pm" for k in (4, 3, 2, 1)]
    + ["yo", "yl"]
    + ["g%s%d" % (d, k) for d in "pm" for k in (1, 2, 3, 4)]
)
NUMBER = {name: i for i, name in enumerate(MESSAGES)}


def rel(dx, dy):
    return (dx % 4) + 4 * dy


def kernel(
    x_hbm, w_hbm, c_hbm, ps_hbm, op_hbm, om_hbm,
    kv_out, grad_out, np_out, nm_out, lw_out,
    Xb, Cb, Wb, TO, T, SB, KVs, KVo, KVr, KVb,
    rap, ram, rd, rbp, rbm, re, rgp, rgm, rhp, rhm, G,
    PSb, zq4p, zq4m, zs, zq, ZS, yr, OPb, OMb, NP, NM, LW,
    ssem, rsem, lsem,
):
    r_id = lax.axis_index("replica")
    f_id = lax.axis_index("fsdp")
    z = lax.rem(r_id, 8)
    ylo = r_id // 8
    c = lax.rem(f_id, 2)
    x = lax.rem(f_id // 2, 4)
    yh = f_id // 8

    def device(x, yh, z, ylo, c):
        return (ylo * 8 + z, yh * 8 + x * 2 + c)

    XP = device(lax.rem(x + 1, 4), yh, z, ylo, c)
    XM = device(lax.rem(x + 3, 4), yh, z, ylo, c)
    Y = device(x, 1 - yh, z, ylo, c)
    YL = device(x, yh, z, 1 - ylo, c)
    ZP = device(x, yh, lax.rem(z + 1, 8), ylo, c)
    ZM = device(x, yh, lax.rem(z + 7, 8), ylo, c)
    SIB = device(x, yh, z, ylo, 1 - c)

    barrier = pltpu.get_barrier_semaphore()
    for dev in (XP, XM, Y, YL, ZP, ZM, SIB):
        pl.semaphore_signal(barrier, inc=1, device_id=dev, device_id_type=MESH)

    def columns(r, core):
        chip = (yh if r < 4 else 1 - yh) * 4 + lax.rem(x + r % 4, 4)
        return pl.ds(pl.multiple_of(chip * 512 + core * 256, 256), 256)

    def lanes(r):
        return pl.ds(r * 256, 256)

    locals_ = []

    def load(src, dst):
        cp = pltpu.make_async_copy(src, dst, lsem.at[len(locals_)])
        cp.start()
        locals_.append(cp)
        return cp

    load_x = [load(x_hbm.at[:, columns(r, c)], Xb.at[0, :, lanes(r)]) for r in range(8)]
    load_c = load(c_hbm, Cb.at[0])
    load_w = load(w_hbm.at[0], Wb.at[0])
    load_ps = []
    for dz in (4, 3, 5, 2, 6, 1, 7, 0):
        for b in range(2):
            cols = pl.ds(pl.multiple_of(b * HALF + lax.rem(z + dz, 8) * FC, FC), FC)
            load_ps.append(load(ps_hbm.at[0, :, cols], PSb.at[dz, b]))
    load_o = [load(op_hbm, OPb), load(om_hbm, OMb)]

    sent = {}

    def send(name, src, dst, dev):
        i = NUMBER[name]
        cp = pltpu.make_async_remote_copy(
            src_ref=src, dst_ref=dst, send_sem=ssem.at[i], recv_sem=rsem.at[i],
            device_id=dev, device_id_type=MESH,
        )
        cp.start()
        sent[name] = cp

    def arrived(*names):
        for name in names:
            sent[name].wait_recv()

    def rows_loop(n, body):
        @pl.loop(0, n // 16)
        def _(i):
            body(lambda base: pl.ds(pl.multiple_of(base + i * 16, 16), 16))

    contract = (((0,), (0,)), ((), ()))

    def own_term(r):
        @pl.loop(0, 2)
        def _(j):
            cols = pl.ds(pl.multiple_of(j * 512, 512), 512)
            TO[r, :, cols] = lax.dot_general(
                Xb[0, :, lanes(r)], Cb[0, :, cols], contract, preferred_element_type=f32
            ).astype(bf16)

    def both_terms(r):
        @pl.loop(0, 2)
        def _(j):
            cols = pl.ds(pl.multiple_of(j * 512, 512), 512)
            other = lax.dot_general(
                Xb[1, :, lanes(r)], Cb[1, :, cols], contract, preferred_element_type=f32
            ).astype(bf16)
            total = TO[r, :, cols].astype(f32) + other.astype(f32)
            T[r, :, cols] = total
            SB[r, :, cols] = total.astype(bf16)

    load_c.wait()
    for cp in load_x:
        cp.wait()
    own_term(rel(2, 0))
    own_term(rel(2, 1))

    pl.semaphore_wait(barrier, 7)

    send("xpP2", w_hbm.at[0, CUT:ROWS], Wb.at[rel(3, 0), CUT:ROWS], XP)
    send("xmP2", w_hbm.at[0, CUT:ROWS], Wb.at[rel(1, 0), CUT:ROWS], XM)
    send("yP1", w_hbm.at[0, 0:CUT], Wb.at[rel(0, 1), 0:CUT], Y)
    send("cs", c_hbm, Cb.at[1], SIB)
    for r in (rel(2, 0), rel(2, 1), rel(1, 1), rel(3, 1), rel(1, 0), rel(3, 0), rel(0, 1), rel(0, 0)):
        send("xs%d" % r, x_hbm.at[:, columns(r, 1 - c)], Xb.at[1, :, lanes(r)], SIB)
    for cp in load_ps:
        cp.wait()
    send("zp4", PSb.at[4, 0], zq4p, ZP)
    send("zm4", PSb.at[4, 1], zq4m, ZM)
    send("xpP1", w_hbm.at[0, 0:CUT], Wb.at[rel(3, 0), 0:CUT], XP)
    send("xmP1", w_hbm.at[0, 0:CUT], Wb.at[rel(1, 0), 0:CUT], XM)
    send("yP2_0", w_hbm.at[0, CUT:ROWS], Wb.at[rel(0, 1), CUT:ROWS], Y)

    def z3():
        arrived("zp4", "zm4")

        def body(at):
            s = at(0)
            zs[0, 0, 0, s] = PSb[3, 0, s].astype(f32) + zq4p[s].astype(f32)
            zs[0, 0, 1, s] = PSb[3, 1, s].astype(f32)
            zs[1, 0, 0, s] = PSb[5, 0, s].astype(f32)
            zs[1, 0, 1, s] = PSb[5, 1, s].astype(f32) + zq4m[s].astype(f32)

        rows_loop(FR, body)
        send("zp3", zs.at[0, 0], zq.at[0, 0], ZP)
        send("zm3", zs.at[1, 0], zq.at[1, 0], ZM)

    def z2():
        arrived("zp3", "zm3")

        def body(at):
            s = at(0)
            for b in range(2):
                zs[0, 1, b, s] = PSb[2, b, s].astype(f32) + zq[0, 0, b, s]
                zs[1, 1, b, s] = PSb[6, b, s].astype(f32) + zq[1, 0, b, s]

        rows_loop(FR, body)
        send("zp2", zs.at[0, 1], zq.at[0, 1], ZP)
        send("zm2", zs.at[1, 1], zq.at[1, 1], ZM)

    def z1():
        arrived("zp2", "zm2")

        def body(at):
            s = at(0)
            for b in range(2):
                zs[0, 2, b, s] = PSb[1, b, s].astype(f32) + zq[0, 1, b, s]
                zs[1, 2, b, s] = PSb[7, b, s].astype(f32) + zq[1, 1, b, s]

        rows_loop(FR, body)
        send("zp1", zs.at[0, 2], zq.at[0, 2], ZP)
        send("zm1", zs.at[1, 2], zq.at[1, 2], ZM)

    def z0():
        arrived("zp1", "zm1")

        def body(at):
            s = at(0)
            for b in range(2):
                ZS[b, s] = PSb[0, b, s].astype(f32) + zq[0, 2, b, s] + zq[1, 2, b, s]

        rows_loop(FR, body)
        send("yo", ZS.at[1 - ylo], yr, YL)

    stores = []

    def store(src, dst):
        cp = pltpu.make_async_copy(src, dst, lsem.at[len(locals_) + len(stores)])
        cp.start()
        stores.append(cp)

    def store_lw(dz, blocks=(0, 1)):
        for b in blocks:
            cols = pl.ds(pl.multiple_of(b * HALF + lax.rem(z + dz, 8) * FC, FC), FC)
            store(LW.at[dz, b], lw_out.at[:, cols])

    def outer_step():
        for cp in load_o:
            cp.wait()
        arrived("yo")

        def body(at):
            s = at(0)
            average = (ZS[ylo, s] + yr[s]) * (1.0 / 16)
            moment = outer_beta * OMb[s] + average
            params = OPb[s] - outer_rate * (outer_beta * moment + average)
            NM[s] = moment
            NP[s] = params
            LW[0, ylo, s] = params.astype(bf16)

        rows_loop(FR, body)
        send("yl", LW.at[0, ylo], LW.at[0, ylo], YL)
        store(NM, nm_out)
        store(NP, np_out)

    def g1():
        arrived("yl")
        send("gp1", LW.at[0], LW.at[7], ZP)
        send("gm1", LW.at[0], LW.at[1], ZM)
        store_lw(0)

    def g2():
        arrived("gp1", "gm1")
        send("gp2", LW.at[7], LW.at[6], ZP)
        send("gm2", LW.at[1], LW.at[2], ZM)
        store_lw(7)
        store_lw(1)

    def g3():
        arrived("gp2", "gm2")
        send("gp3", LW.at[6], LW.at[5], ZP)
        send("gm3", LW.at[2], LW.at[3], ZM)
        store_lw(6)
        store_lw(2)

    def g4():
        arrived("gp3", "gm3")
        send("gp4", LW.at[5, 0], LW.at[4, 0], ZP)
        send("gm4", LW.at[3, 1], LW.at[4, 1], ZM)
        store_lw(5)
        store_lw(3)

    def g5():
        arrived("gp4", "gm4")
        store_lw(4)

    def a_p2():
        arrived("xpP2", "xmP2")
        send("xpfP2", Wb.at[rel(3, 0), CUT:MID2], Wb.at[rel(2, 0), CUT:MID2], XP)
        send("xmfP2", Wb.at[rel(1, 0), MID2:ROWS], Wb.at[rel(2, 0), MID2:ROWS], XM)
        send("yP2_3", Wb.at[rel(3, 0), CUT:ROWS], Wb.at[rel(3, 1), CUT:ROWS], Y)
        send("yP2_1", Wb.at[rel(1, 0), CUT:ROWS], Wb.at[rel(1, 1), CUT:ROWS], Y)

    def a_q1():
        arrived("yP1")
        send("xpQ1", Wb.at[rel(0, 1), 0:CUT], Wb.at[rel(3, 1), 0:CUT], XP)
        send("xmQ1", Wb.at[rel(0, 1), 0:CUT], Wb.at[rel(1, 1), 0:CUT], XM)

    def a_p1():
        arrived("xpP1", "xmP1")
        send("xpfP1", Wb.at[rel(3, 0), 0:MID1], Wb.at[rel(2, 0), 0:MID1], XP)
        send("xmfP1", Wb.at[rel(1, 0), MID1:CUT], Wb.at[rel(2, 0), MID1:CUT], XM)

    def a_p2far():
        arrived("xpfP2", "xmfP2")
        send("yP2_2a", Wb.at[rel(2, 0), CUT:MID2], Wb.at[rel(2, 1), CUT:MID2], Y)
        send("yP2_2b", Wb.at[rel(2, 0), MID2:ROWS], Wb.at[rel(2, 1), MID2:ROWS], Y)

    def a_fq1():
        arrived("xpQ1", "xmQ1")
        send("xpfQ1", Wb.at[rel(3, 1), 0:MID1], Wb.at[rel(2, 1), 0:MID1], XP)
        send("xmfQ1", Wb.at[rel(1, 1), MID1:CUT], Wb.at[rel(2, 1), MID1:CUT], XM)

    def b_send(dy):
        r = rel(2, dy)
        send("bp%d" % dy, SB.at[r, 0:MID1], rap.at[dy], XP)
        send("bm%d" % dy, SB.at[r, MID1:CUT], ram.at[dy], XM)

    def d_send(dx):
        send("d%d" % dx, SB.at[rel(dx, 1), CUT:ROWS], rd.at[dx], Y)

    def c_plain(dx, dy):
        if dx == 1:
            send("cp%db" % dy, SB.at[rel(1, dy), MID1:CUT], rbp.at[dy, MID1:CUT], XP)
        else:
            send("cm%db" % dy, SB.at[rel(3, dy), 0:MID1], rbm.at[dy, 0:MID1], XM)

    def c_added(dy):
        arrived("bp%d" % dy, "bm%d" % dy)

        def body(at):
            s, t = at(0), at(MID1)
            SB[rel(1, dy), s] = (T[rel(1, dy), s] + rap[dy, s].astype(f32)).astype(bf16)
            SB[rel(3, dy), t] = (T[rel(3, dy), t] + ram[dy, s].astype(f32)).astype(bf16)

        rows_loop(MID1, body)
        send("cp%da" % dy, SB.at[rel(1, dy), 0:MID1], rbp.at[dy, 0:MID1], XP)
        send("cm%da" % dy, SB.at[rel(3, dy), MID1:CUT], rbm.at[dy, MID1:CUT], XM)

    def e_send():
        arrived("cp1a", "cp1b", "cm1a", "cm1b")

        def body(at):
            s = at(0)
            total = T[rel(0, 1), s] + rbp[1, s].astype(f32) + rbm[1, s].astype(f32)
            SB[rel(0, 1), s] = total.astype(bf16)

        rows_loop(CUT, body)
        send("e", SB.at[rel(0, 1), 0:CUT], re, Y)

    def g_send():
        arrived("d2")

        def body(at):
            s, t = at(0), at(CUT)
            SB[rel(2, 0), t] = (T[rel(2, 0), t] + rd[2, s].astype(f32)).astype(bf16)

        rows_loop(ROWS - CUT, body)
        send("gp", SB.at[rel(2, 0), CUT:MID2], rgp, XP)
        send("gm", SB.at[rel(2, 0), MID2:ROWS], rgm, XM)

    def h_send():
        arrived("d1", "d3", "gp", "gm")
        half = MID2 - CUT

        def body(at):
            s, u, t, v = at(0), at(half), at(CUT), at(MID2)
            SB[rel(1, 0), t] = (T[rel(1, 0), t] + rd[1, s].astype(f32) + rgp[s].astype(f32)).astype(bf16)
            SB[rel(1, 0), v] = (T[rel(1, 0), v] + rd[1, u].astype(f32)).astype(bf16)
            SB[rel(3, 0), t] = (T[rel(3, 0), t] + rd[3, s].astype(f32)).astype(bf16)
            SB[rel(3, 0), v] = (T[rel(3, 0), v] + rd[3, u].astype(f32) + rgm[s].astype(f32)).astype(bf16)

        rows_loop(half, body)
        send("hp", SB.at[rel(1, 0), CUT:ROWS], rhp, XP)
        send("hm", SB.at[rel(3, 0), CUT:ROWS], rhm, XM)

    def finish_high():
        arrived("d0", "hp", "hm")

        def body(at):
            s, t = at(0), at(CUT)
            G[t] = T[rel(0, 0), t] + rd[0, s].astype(f32) + rhp[s].astype(f32) + rhm[s].astype(f32)

        rows_loop(ROWS - CUT, body)
        store(G.at[CUT:ROWS], grad_out.at[0, CUT:ROWS])

    def finish_low():
        arrived("cp0a", "cp0b", "cm0a", "cm0b")

        def body(at):
            s = at(0)
            G[s] = T[rel(0, 0), s] + rbp[0, s].astype(f32) + rbm[0, s].astype(f32)

        rows_loop(CUT, body)
        arrived("e")

        def body2(at):
            s = at(0)
            G[s] = G[s] + re[s].astype(f32)

        rows_loop(CUT, body2)
        store(G.at[0:CUT], grad_out.at[0, 0:CUT])

    def kv_part(slot, dst):
        for h in range(2):
            @pl.loop(0, 2)
            def _(j):
                cols = pl.ds(pl.multiple_of(h * 512 + j * 256, 256), 256)
                weights = Wb[:, :, cols].reshape(HALF, 256)
                dst[:, cols] = jnp.dot(Xb[slot], weights, preferred_element_type=f32)

            if slot == 1:
                cols = slice(h * 512, h * 512 + 512)
                send("kv%d" % h, KVs.at[:, cols], KVr.at[:, cols], SIB)

    def kv_compute():
        load_w.wait()
        arrived("yP2_0", "yP2_1", "yP2_3", "yP2_2a", "yP2_2b", "xpfP1", "xmfP1", "xpfQ1", "xmfQ1")
        kv_part(1, KVs)
        kv_part(0, KVo)

    def kv_finish():
        arrived("kv0", "kv1")

        def body(at):
            s = at(0)
            KVb[s] = (KVo[s] + KVr[s]).astype(bf16)

        rows_loop(TOK, body)
        store(KVb, kv_out)

    own_term(rel(1, 1))
    own_term(rel(3, 1))
    z3()
    arrived("cs", "xs%d" % rel(2, 0), "xs%d" % rel(2, 1))
    both_terms(rel(2, 0))
    both_terms(rel(2, 1))
    b_send(0)
    b_send(1)
    d_send(2)
    a_p2()
    a_q1()
    own_term(rel(1, 0))
    own_term(rel(3, 0))
    arrived(*["xs%d" % rel(dx, dy) for dx, dy in ((1, 1), (3, 1), (1, 0), (3, 0), (0, 1), (0, 0))])
    for dx, dy in ((1, 1), (3, 1), (1, 0), (3, 0)):
        both_terms(rel(dx, dy))
        c_plain(dx, dy)
        if dy == 1:
            d_send(dx)
    a_p1()
    z2()
    own_term(rel(0, 1))
    own_term(rel(0, 0))
    both_terms(rel(0, 1))
    d_send(0)
    both_terms(rel(0, 0))
    a_p2far()
    z1()
    a_fq1()
    c_added(1)
    c_added(0)
    g_send()
    z0()
    outer_step()
    kv_compute()
    g1()
    h_send()
    e_send()
    g2()
    kv_finish()
    g3()
    finish_high()
    g4()
    finish_low()
    g5()

    for cp in sent.values():
        cp.wait_send()
    for cp in stores:
        cp.wait()


def on_device(inputs, projection, cotangent, pseudo_grad, outer_params, outer_momentum):
    any_ = pl.BlockSpec(memory_space=pl.ANY)
    vm = pltpu.VMEM
    scratch = [
        vm((2, TOK, HALF), bf16),
        vm((2, TOK, KV), bf16),
        vm((8, ROWS, KV), bf16),
        vm((8, ROWS, KV), bf16),
        vm((8, ROWS, KV), f32),
        vm((8, ROWS, KV), bf16),
        vm((TOK, KV), f32),
        vm((TOK, KV), f32),
        vm((TOK, KV), f32),
        vm((TOK, KV), bf16),
        vm((2, MID1, KV), bf16),
        vm((2, MID1, KV), bf16),
        vm((4, ROWS - CUT, KV), bf16),
        vm((2, CUT, KV), bf16),
        vm((2, CUT, KV), bf16),
        vm((CUT, KV), bf16),
        vm((MID2 - CUT, KV), bf16),
        vm((MID2 - CUT, KV), bf16),
        vm((ROWS - CUT, KV), bf16),
        vm((ROWS - CUT, KV), bf16),
        vm((ROWS, KV), f32),
        vm((8, 2, FR, FC), bf16),
        vm((FR, FC), bf16),
        vm((FR, FC), bf16),
        vm((2, 3, 2, FR, FC), f32),
        vm((2, 3, 2, FR, FC), f32),
        vm((2, FR, FC), f32),
        vm((FR, FC), f32),
        vm((FR, FC), f32),
        vm((FR, FC), f32),
        vm((FR, FC), f32),
        vm((FR, FC), f32),
        vm((8, 2, FR, FC), bf16),
        pltpu.SemaphoreType.DMA((len(MESSAGES),)),
        pltpu.SemaphoreType.DMA((len(MESSAGES),)),
        pltpu.SemaphoreType.DMA((64,)),
    ]
    return pl.pallas_call(
        kernel,
        out_shape=(
            jax.ShapeDtypeStruct((TOK, KV), bf16),
            jax.ShapeDtypeStruct((1, ROWS, KV), f32),
            jax.ShapeDtypeStruct((FR, FC), f32),
            jax.ShapeDtypeStruct((FR, FC), f32),
            jax.ShapeDtypeStruct((FR, D), bf16),
        ),
        in_specs=[any_] * 6,
        out_specs=(any_,) * 5,
        scratch_shapes=scratch,
        compiler_params=pltpu.CompilerParams(
            collective_id=0, has_side_effects=True, vmem_limit_bytes=60 * 2**20
        ),
        cost_estimate=pl.CostEstimate(flops=6 * 10**9, bytes_accessed=3 * 10**7, transcendentals=0),
    )(inputs, projection, cotangent, pseudo_grad, outer_params, outer_momentum)


def solution(mesh):
    return jax.shard_map(
        on_device,
        mesh=mesh,
        in_specs=(
            P(("replica", "fsdp"), None),
            P("replica", "fsdp", None),
            P(("replica", "fsdp"), None),
            P("replica", "fsdp", None),
            P("fsdp", "replica"),
            P("fsdp", "replica"),
        ),
        out_specs=(
            P(("replica", "fsdp"), None),
            P("replica", "fsdp", None),
            P("fsdp", "replica"),
            P("fsdp", "replica"),
            P("fsdp", None),
        ),
        check_vma=False,
    )
```

```python
import jax
import jax.numpy as jnp
from jax import lax
from jax.experimental import pallas as pl
from jax.experimental.pallas import tpu as pltpu
from jax.sharding import PartitionSpec as P

outer_rate = 0.7
outer_beta = 0.9

MESH = pl.DeviceIdType.MESH
bf16 = jnp.bfloat16
f32 = jnp.float32

TOK = 384
D = 4096
HALF = 2048
KV = 1024
ROWS = 256
CUT = 160
MID1 = CUT // 2
MID2 = CUT + (ROWS - CUT) // 2
FR = 128
FC = 256

MESSAGES = (
    ["yP1", "yP2_0", "yP2_1", "yP2_3", "yP2_2a", "yP2_2b"]
    + [d + k for d in ("xp", "xm") for k in ("P2", "P1", "Q1", "fP2", "fP1", "fQ1")]
    + ["xs%d" % r for r in range(8)]
    + ["cs", "kv0", "kv1"]
    + ["b%s%d" % (d, y) for d in "pm" for y in (0, 1)]
    + ["c%s%d%s" % (d, y, h) for d in "pm" for y in (0, 1) for h in "ab"]
    + ["d%d" % x for x in range(4)]
    + ["e", "gp", "gm", "hp", "hm"]
    + ["z%s%d" % (d, k) for d in "pm" for k in (4, 3, 2, 1)]
    + ["yo", "yl"]
    + ["g%s%d" % (d, k) for d in "pm" for k in (1, 2, 3, 4)]
)
NUMBER = {name: i for i, name in enumerate(MESSAGES)}


def rel(dx, dy):
    return (dx % 4) + 4 * dy


def kernel(
    x_hbm, w_hbm, c_hbm, ps_hbm, op_hbm, om_hbm,
    KVb, G, NP, NM, LW,
    Xb, Cb, Wb, TO, T, SB, KVs, KVo, KVr,
    rap, ram, rd, rbp, rbm, re, rgp, rgm, rhp, rhm,
    PSb, zq4p, zq4m, zs, zq, ZS, yr, OPb, OMb,
    ssem, rsem, lsem,
):
    r_id = lax.axis_index("replica")
    f_id = lax.axis_index("fsdp")
    z = lax.rem(r_id, 8)
    ylo = r_id // 8
    c = lax.rem(f_id, 2)
    x = lax.rem(f_id // 2, 4)
    yh = f_id // 8

    def device(x, yh, z, ylo, c):
        return (ylo * 8 + z, yh * 8 + x * 2 + c)

    XP = device(lax.rem(x + 1, 4), yh, z, ylo, c)
    XM = device(lax.rem(x + 3, 4), yh, z, ylo, c)
    Y = device(x, 1 - yh, z, ylo, c)
    YL = device(x, yh, z, 1 - ylo, c)
    ZP = device(x, yh, lax.rem(z + 1, 8), ylo, c)
    ZM = device(x, yh, lax.rem(z + 7, 8), ylo, c)
    SIB = device(x, yh, z, ylo, 1 - c)

    barrier = pltpu.get_barrier_semaphore()
    for dev in (XP, XM, Y, YL, ZP, ZM, SIB):
        pl.semaphore_signal(barrier, inc=1, device_id=dev, device_id_type=MESH)

    def columns(r, core):
        chip = (yh if r < 4 else 1 - yh) * 4 + lax.rem(x + r % 4, 4)
        return pl.ds(pl.multiple_of(chip * 512 + core * 256, 256), 256)

    def lanes(r):
        return pl.ds(r * 256, 256)

    locals_ = []

    def load(src, dst):
        cp = pltpu.make_async_copy(src, dst, lsem.at[len(locals_)])
        cp.start()
        locals_.append(cp)
        return cp

    load_x = [load(x_hbm.at[:, columns(r, c)], Xb.at[0, :, lanes(r)]) for r in range(8)]
    load_c = load(c_hbm, Cb.at[0])
    load_w = load(w_hbm.at[0], Wb.at[0])
    load_ps = []
    for dz in (4, 3, 5, 2, 6, 1, 7, 0):
        for b in range(2):
            cols = pl.ds(pl.multiple_of(b * HALF + lax.rem(z + dz, 8) * FC, FC), FC)
            load_ps.append(load(ps_hbm.at[0, :, cols], PSb.at[dz, b]))
    load_o = [load(op_hbm, OPb), load(om_hbm, OMb)]

    sent = {}

    def send(name, src, dst, dev):
        i = NUMBER[name]
        cp = pltpu.make_async_remote_copy(
            src_ref=src, dst_ref=dst, send_sem=ssem.at[i], recv_sem=rsem.at[i],
            device_id=dev, device_id_type=MESH,
        )
        cp.start()
        sent[name] = cp

    def arrived(*names):
        for name in names:
            sent[name].wait_recv()

    def rows_loop(n, body):
        @pl.loop(0, n // 16)
        def _(i):
            body(lambda base: pl.ds(pl.multiple_of(base + i * 16, 16), 16))

    contract = (((0,), (0,)), ((), ()))

    def own_term(r):
        @pl.loop(0, 2)
        def _(j):
            cols = pl.ds(pl.multiple_of(j * 512, 512), 512)
            TO[r, :, cols] = lax.dot_general(
                Xb[0, :, lanes(r)], Cb[0, :, cols], contract, preferred_element_type=f32
            ).astype(bf16)

    def both_terms(r):
        @pl.loop(0, 2)
        def _(j):
            cols = pl.ds(pl.multiple_of(j * 512, 512), 512)
            other = lax.dot_general(
                Xb[1, :, lanes(r)], Cb[1, :, cols], contract, preferred_element_type=f32
            ).astype(bf16)
            total = TO[r, :, cols].astype(f32) + other.astype(f32)
            T[r, :, cols] = total
            SB[r, :, cols] = total.astype(bf16)

    load_c.wait()
    for cp in load_x:
        cp.wait()
    own_term(rel(2, 0))
    own_term(rel(2, 1))

    pl.semaphore_wait(barrier, 7)

    send("xpP2", w_hbm.at[0, CUT:ROWS], Wb.at[rel(3, 0), CUT:ROWS], XP)
    send("xmP2", w_hbm.at[0, CUT:ROWS], Wb.at[rel(1, 0), CUT:ROWS], XM)
    send("yP1", w_hbm.at[0, 0:CUT], Wb.at[rel(0, 1), 0:CUT], Y)
    send("cs", c_hbm, Cb.at[1], SIB)
    for r in (rel(2, 0), rel(2, 1), rel(1, 1), rel(3, 1), rel(1, 0), rel(3, 0), rel(0, 1), rel(0, 0)):
        send("xs%d" % r, x_hbm.at[:, columns(r, 1 - c)], Xb.at[1, :, lanes(r)], SIB)
    for cp in load_ps:
        cp.wait()
    send("zp4", PSb.at[4, 0], zq4p, ZP)
    send("zm4", PSb.at[4, 1], zq4m, ZM)
    send("xpP1", w_hbm.at[0, 0:CUT], Wb.at[rel(3, 0), 0:CUT], XP)
    send("xmP1", w_hbm.at[0, 0:CUT], Wb.at[rel(1, 0), 0:CUT], XM)
    send("yP2_0", w_hbm.at[0, CUT:ROWS], Wb.at[rel(0, 1), CUT:ROWS], Y)

    def z3():
        arrived("zp4", "zm4")

        def body(at):
            s = at(0)
            zs[0, 0, 0, s] = PSb[3, 0, s].astype(f32) + zq4p[s].astype(f32)
            zs[0, 0, 1, s] = PSb[3, 1, s].astype(f32)
            zs[1, 0, 0, s] = PSb[5, 0, s].astype(f32)
            zs[1, 0, 1, s] = PSb[5, 1, s].astype(f32) + zq4m[s].astype(f32)

        rows_loop(FR, body)
        send("zp3", zs.at[0, 0], zq.at[0, 0], ZP)
        send("zm3", zs.at[1, 0], zq.at[1, 0], ZM)

    def z2():
        arrived("zp3", "zm3")

        def body(at):
            s = at(0)
            for b in range(2):
                zs[0, 1, b, s] = PSb[2, b, s].astype(f32) + zq[0, 0, b, s]
                zs[1, 1, b, s] = PSb[6, b, s].astype(f32) + zq[1, 0, b, s]

        rows_loop(FR, body)
        send("zp2", zs.at[0, 1], zq.at[0, 1], ZP)
        send("zm2", zs.at[1, 1], zq.at[1, 1], ZM)

    def z1():
        arrived("zp2", "zm2")

        def body(at):
            s = at(0)
            for b in range(2):
                zs[0, 2, b, s] = PSb[1, b, s].astype(f32) + zq[0, 1, b, s]
                zs[1, 2, b, s] = PSb[7, b, s].astype(f32) + zq[1, 1, b, s]

        rows_loop(FR, body)
        send("zp1", zs.at[0, 2], zq.at[0, 2], ZP)
        send("zm1", zs.at[1, 2], zq.at[1, 2], ZM)

    def z0():
        arrived("zp1", "zm1")

        def body(at):
            s = at(0)
            for b in range(2):
                ZS[b, s] = PSb[0, b, s].astype(f32) + zq[0, 2, b, s] + zq[1, 2, b, s]

        rows_loop(FR, body)
        send("yo", ZS.at[1 - ylo], yr, YL)

    def outer_step():
        for cp in load_o:
            cp.wait()
        arrived("yo")

        def body(at):
            s = at(0)
            average = (ZS[ylo, s] + yr[s]) * (1.0 / 16)
            moment = outer_beta * OMb[s] + average
            params = OPb[s] - outer_rate * (outer_beta * moment + average)
            NM[s] = moment
            NP[s] = params
            LW[0, ylo, s] = params.astype(bf16)

        rows_loop(FR, body)
        send("yl", LW.at[0, ylo], LW.at[0, ylo], YL)

    def g1():
        arrived("yl")
        send("gp1", LW.at[0], LW.at[7], ZP)
        send("gm1", LW.at[0], LW.at[1], ZM)

    def g2():
        arrived("gp1", "gm1")
        send("gp2", LW.at[7], LW.at[6], ZP)
        send("gm2", LW.at[1], LW.at[2], ZM)

    def g3():
        arrived("gp2", "gm2")
        send("gp3", LW.at[6], LW.at[5], ZP)
        send("gm3", LW.at[2], LW.at[3], ZM)

    def g4():
        arrived("gp3", "gm3")
        send("gp4", LW.at[5, 0], LW.at[4, 0], ZP)
        send("gm4", LW.at[3, 1], LW.at[4, 1], ZM)

    def g5():
        arrived("gp4", "gm4")

    def a_p2():
        arrived("xpP2", "xmP2")
        send("xpfP2", Wb.at[rel(3, 0), CUT:MID2], Wb.at[rel(2, 0), CUT:MID2], XP)
        send("xmfP2", Wb.at[rel(1, 0), MID2:ROWS], Wb.at[rel(2, 0), MID2:ROWS], XM)
        send("yP2_3", Wb.at[rel(3, 0), CUT:ROWS], Wb.at[rel(3, 1), CUT:ROWS], Y)
        send("yP2_1", Wb.at[rel(1, 0), CUT:ROWS], Wb.at[rel(1, 1), CUT:ROWS], Y)

    def a_q1():
        arrived("yP1")
        send("xpQ1", Wb.at[rel(0, 1), 0:CUT], Wb.at[rel(3, 1), 0:CUT], XP)
        send("xmQ1", Wb.at[rel(0, 1), 0:CUT], Wb.at[rel(1, 1), 0:CUT], XM)

    def a_p1():
        arrived("xpP1", "xmP1")
        send("xpfP1", Wb.at[rel(3, 0), 0:MID1], Wb.at[rel(2, 0), 0:MID1], XP)
        send("xmfP1", Wb.at[rel(1, 0), MID1:CUT], Wb.at[rel(2, 0), MID1:CUT], XM)

    def a_p2far():
        arrived("xpfP2", "xmfP2")
        send("yP2_2a", Wb.at[rel(2, 0), CUT:MID2], Wb.at[rel(2, 1), CUT:MID2], Y)
        send("yP2_2b", Wb.at[rel(2, 0), MID2:ROWS], Wb.at[rel(2, 1), MID2:ROWS], Y)

    def a_fq1():
        arrived("xpQ1", "xmQ1")
        send("xpfQ1", Wb.at[rel(3, 1), 0:MID1], Wb.at[rel(2, 1), 0:MID1], XP)
        send("xmfQ1", Wb.at[rel(1, 1), MID1:CUT], Wb.at[rel(2, 1), MID1:CUT], XM)

    def b_send(dy):
        r = rel(2, dy)
        send("bp%d" % dy, SB.at[r, 0:MID1], rap.at[dy], XP)
        send("bm%d" % dy, SB.at[r, MID1:CUT], ram.at[dy], XM)

    def d_send(dx):
        send("d%d" % dx, SB.at[rel(dx, 1), CUT:ROWS], rd.at[dx], Y)

    def c_plain(dx, dy):
        if dx == 1:
            send("cp%db" % dy, SB.at[rel(1, dy), MID1:CUT], rbp.at[dy, MID1:CUT], XP)
        else:
            send("cm%db" % dy, SB.at[rel(3, dy), 0:MID1], rbm.at[dy, 0:MID1], XM)

    def c_added(dy):
        arrived("bp%d" % dy, "bm%d" % dy)

        def body(at):
            s, t = at(0), at(MID1)
            SB[rel(1, dy), s] = (T[rel(1, dy), s] + rap[dy, s].astype(f32)).astype(bf16)
            SB[rel(3, dy), t] = (T[rel(3, dy), t] + ram[dy, s].astype(f32)).astype(bf16)

        rows_loop(MID1, body)
        send("cp%da" % dy, SB.at[rel(1, dy), 0:MID1], rbp.at[dy, 0:MID1], XP)
        send("cm%da" % dy, SB.at[rel(3, dy), MID1:CUT], rbm.at[dy, MID1:CUT], XM)

    def e_send():
        arrived("cp1a", "cp1b", "cm1a", "cm1b")

        def body(at):
            s = at(0)
            total = T[rel(0, 1), s] + rbp[1, s].astype(f32) + rbm[1, s].astype(f32)
            SB[rel(0, 1), s] = total.astype(bf16)

        rows_loop(CUT, body)
        send("e", SB.at[rel(0, 1), 0:CUT], re, Y)

    def g_send():
        arrived("d2")

        def body(at):
            s, t = at(0), at(CUT)
            SB[rel(2, 0), t] = (T[rel(2, 0), t] + rd[2, s].astype(f32)).astype(bf16)

        rows_loop(ROWS - CUT, body)
        send("gp", SB.at[rel(2, 0), CUT:MID2], rgp, XP)
        send("gm", SB.at[rel(2, 0), MID2:ROWS], rgm, XM)

    def h_send():
        arrived("d1", "d3", "gp", "gm")
        half = MID2 - CUT

        def body(at):
            s, u, t, v = at(0), at(half), at(CUT), at(MID2)
            SB[rel(1, 0), t] = (T[rel(1, 0), t] + rd[1, s].astype(f32) + rgp[s].astype(f32)).astype(bf16)
            SB[rel(1, 0), v] = (T[rel(1, 0), v] + rd[1, u].astype(f32)).astype(bf16)
            SB[rel(3, 0), t] = (T[rel(3, 0), t] + rd[3, s].astype(f32)).astype(bf16)
            SB[rel(3, 0), v] = (T[rel(3, 0), v] + rd[3, u].astype(f32) + rgm[s].astype(f32)).astype(bf16)

        rows_loop(half, body)
        send("hp", SB.at[rel(1, 0), CUT:ROWS], rhp, XP)
        send("hm", SB.at[rel(3, 0), CUT:ROWS], rhm, XM)

    def finish_high():
        arrived("d0", "hp", "hm")

        def body(at):
            s, t = at(0), at(CUT)
            G[t] = T[rel(0, 0), t] + rd[0, s].astype(f32) + rhp[s].astype(f32) + rhm[s].astype(f32)

        rows_loop(ROWS - CUT, body)

    def finish_low():
        arrived("cp0a", "cp0b", "cm0a", "cm0b")

        def body(at):
            s = at(0)
            G[s] = T[rel(0, 0), s] + rbp[0, s].astype(f32) + rbm[0, s].astype(f32)

        rows_loop(CUT, body)
        arrived("e")

        def body2(at):
            s = at(0)
            G[s] = G[s] + re[s].astype(f32)

        rows_loop(CUT, body2)

    def kv_part(slot, dst):
        for h in range(2):
            @pl.loop(0, 2)
            def _(j):
                cols = pl.ds(pl.multiple_of(h * 512 + j * 256, 256), 256)
                weights = Wb[:, :, cols].reshape(HALF, 256)
                dst[:, cols] = jnp.dot(Xb[slot], weights, preferred_element_type=f32)

            if slot == 1:
                cols = slice(h * 512, h * 512 + 512)
                send("kv%d" % h, KVs.at[:, cols], KVr.at[:, cols], SIB)

    def kv_wait():
        load_w.wait()
        arrived("yP2_0", "yP2_1", "yP2_3", "yP2_2a", "yP2_2b", "xpfP1", "xmfP1", "xpfQ1", "xmfQ1")

    def kv_finish():
        arrived("kv0", "kv1")

        def body(at):
            s = at(0)
            KVb[s] = (KVo[s] + KVr[s]).astype(bf16)

        rows_loop(TOK, body)

    own_term(rel(1, 1))
    own_term(rel(3, 1))
    z3()
    own_term(rel(1, 0))
    own_term(rel(3, 0))
    arrived("cs", *["xs%d" % r for r in range(8)])
    both_terms(rel(2, 1))
    a_p2()
    both_terms(rel(2, 0))
    own_term(rel(0, 1))
    own_term(rel(0, 0))
    a_q1()
    z2()
    both_terms(rel(1, 1))
    both_terms(rel(3, 1))
    a_p1()
    b_send(1)
    a_p2far()
    d_send(2)
    both_terms(rel(1, 0))
    both_terms(rel(3, 0))
    both_terms(rel(0, 1))
    both_terms(rel(0, 0))
    z1()
    a_fq1()
    z0()
    d_send(1)
    c_added(1)
    c_plain(1, 1)
    c_plain(3, 1)
    b_send(0)
    outer_step()
    d_send(3)
    g_send()
    c_plain(1, 0)
    c_plain(3, 0)
    kv_wait()
    kv_part(1, KVs)
    g1()
    kv_part(0, KVo)
    e_send()
    d_send(0)
    g2()
    c_added(0)
    h_send()
    g3()
    kv_finish()
    g4()
    finish_low()
    g5()
    finish_high()

    for cp in sent.values():
        cp.wait_send()


def write_out(kv, grad, params, moment, weights, kv_out, grad_out, np_out, nm_out, lw_out, sem):
    z = lax.rem(lax.axis_index("replica"), 8)
    pairs = [(kv, kv_out), (grad, grad_out.at[0]), (params, np_out), (moment, nm_out)]
    for dz in range(8):
        for b in range(2):
            cols = pl.ds(pl.multiple_of(b * HALF + lax.rem(z + dz, 8) * FC, FC), FC)
            pairs.append((weights.at[dz, b], lw_out.at[:, cols]))
    copies = [pltpu.make_async_copy(src, dst, sem.at[i]) for i, (src, dst) in enumerate(pairs)]
    for cp in copies:
        cp.start()
    for cp in copies:
        cp.wait()


def on_device(inputs, projection, cotangent, pseudo_grad, outer_params, outer_momentum):
    any_ = pl.BlockSpec(memory_space=pl.ANY)
    inside = pl.BlockSpec(memory_space=pltpu.VMEM)
    vm = pltpu.VMEM
    scratch = [
        vm((2, TOK, HALF), bf16),
        vm((2, TOK, KV), bf16),
        vm((8, ROWS, KV), bf16),
        vm((8, ROWS, KV), bf16),
        vm((8, ROWS, KV), f32),
        vm((8, ROWS, KV), bf16),
        vm((TOK, KV), f32),
        vm((TOK, KV), f32),
        vm((TOK, KV), f32),
        vm((2, MID1, KV), bf16),
        vm((2, MID1, KV), bf16),
        vm((4, ROWS - CUT, KV), bf16),
        vm((2, CUT, KV), bf16),
        vm((2, CUT, KV), bf16),
        vm((CUT, KV), bf16),
        vm((MID2 - CUT, KV), bf16),
        vm((MID2 - CUT, KV), bf16),
        vm((ROWS - CUT, KV), bf16),
        vm((ROWS - CUT, KV), bf16),
        vm((8, 2, FR, FC), bf16),
        vm((FR, FC), bf16),
        vm((FR, FC), bf16),
        vm((2, 3, 2, FR, FC), f32),
        vm((2, 3, 2, FR, FC), f32),
        vm((2, FR, FC), f32),
        vm((FR, FC), f32),
        vm((FR, FC), f32),
        vm((FR, FC), f32),
        pltpu.SemaphoreType.DMA((len(MESSAGES),)),
        pltpu.SemaphoreType.DMA((len(MESSAGES),)),
        pltpu.SemaphoreType.DMA((64,)),
    ]
    operands = (inputs, projection, cotangent, pseudo_grad, outer_params, outer_momentum)
    operands = [pltpu.with_memory_space_constraint(a, pltpu.HBM) for a in operands]
    results = pl.pallas_call(
        kernel,
        out_shape=(
            vm((TOK, KV), bf16),
            vm((ROWS, KV), f32),
            vm((FR, FC), f32),
            vm((FR, FC), f32),
            vm((8, 2, FR, FC), bf16),
        ),
        in_specs=[any_] * 6,
        out_specs=(inside,) * 5,
        scratch_shapes=scratch,
        compiler_params=pltpu.CompilerParams(
            collective_id=0, has_side_effects=True, vmem_limit_bytes=44 * 2**20
        ),
        cost_estimate=pl.CostEstimate(flops=6 * 10**9, bytes_accessed=3 * 10**7, transcendentals=0),
    )(*operands)
    results = [pltpu.with_memory_space_constraint(a, pltpu.VMEM) for a in results]
    return pl.pallas_call(
        write_out,
        out_shape=(
            jax.ShapeDtypeStruct((TOK, KV), bf16),
            jax.ShapeDtypeStruct((1, ROWS, KV), f32),
            jax.ShapeDtypeStruct((FR, FC), f32),
            jax.ShapeDtypeStruct((FR, FC), f32),
            jax.ShapeDtypeStruct((FR, D), bf16),
        ),
        in_specs=[inside] * 5,
        out_specs=(any_,) * 5,
        scratch_shapes=[pltpu.SemaphoreType.DMA((20,))],
        compiler_params=pltpu.CompilerParams(vmem_limit_bytes=44 * 2**20),
    )(*results)


def solution(mesh):
    return jax.shard_map(
        on_device,
        mesh=mesh,
        in_specs=(
            P(("replica", "fsdp"), None),
            P("replica", "fsdp", None),
            P(("replica", "fsdp"), None),
            P("replica", "fsdp", None),
            P("fsdp", "replica"),
            P("fsdp", "replica"),
        ),
        out_specs=(
            P(("replica", "fsdp"), None),
            P("replica", "fsdp", None),
            P("fsdp", "replica"),
            P("fsdp", "replica"),
            P("fsdp", None),
        ),
        check_vma=False,
    )
```

```python
import jax
import jax.numpy as jnp
from jax import lax
from jax.experimental import pallas as pl
from jax.experimental.pallas import tpu as pltpu
from jax.sharding import PartitionSpec as P

outer_rate = 0.7
outer_beta = 0.9

MESH = pl.DeviceIdType.MESH
bf16 = jnp.bfloat16
f32 = jnp.float32

TOK = 384
D = 4096
HALF = 2048
KV = 1024
ROWS = 256
CUT = 160
MID1 = CUT // 2
MID2 = CUT + (ROWS - CUT) // 2
FR = 128
FC = 256

MESSAGES = (
    ["yP1", "yP2_0", "yP2_1", "yP2_3", "yP2_2a", "yP2_2b"]
    + [d + k for d in ("xp", "xm") for k in ("P2", "P1", "Q1", "fP2", "fP1", "fQ1")]
    + ["xs%d" % r for r in range(8)]
    + ["cs", "kv0", "kv1"]
    + ["b%s%d" % (d, y) for d in "pm" for y in (0, 1)]
    + ["c%s%d%s" % (d, y, h) for d in "pm" for y in (0, 1) for h in "ab"]
    + ["d%d" % x for x in range(4)]
    + ["e", "gp", "gm", "hp", "hm"]
    + ["z%s%s" % (d, k) for d in "pm" for k in ("L4", "S3", "L3", "S2", "L2", "S1", "L1")]
    + ["yo", "yl"]
    + ["g%s%s%d" % (d, k, n) for d in "pm" for k in "oq" for n in (1, 2, 3)]
    + ["gpo4", "gmq4"]
)
NUMBER = {name: i for i, name in enumerate(MESSAGES)}


def rel(dx, dy):
    return (dx % 4) + 4 * dy


def kernel(
    x_hbm, w_hbm, c_hbm, ps_hbm, op_hbm, om_hbm,
    KVb, G, NP, NM, LW,
    Xb, Cb, Wb, TO, T, SB, KVs, KVo, KVr,
    rap, ram, rd, rbp, rbm, re, rgp, rgm, rhp, rhm,
    PSb, zraw, zout, zin, ZS, yr, OPb, OMb,
    ssem, rsem, lsem, zsem,
):
    r_id = lax.axis_index("replica")
    f_id = lax.axis_index("fsdp")
    z = lax.rem(r_id, 8)
    ylo = r_id // 8
    c = lax.rem(f_id, 2)
    x = lax.rem(f_id // 2, 4)
    yh = f_id // 8

    def device(x, yh, z, ylo, c):
        return (ylo * 8 + z, yh * 8 + x * 2 + c)

    XP = device(lax.rem(x + 1, 4), yh, z, ylo, c)
    XM = device(lax.rem(x + 3, 4), yh, z, ylo, c)
    Y = device(x, 1 - yh, z, ylo, c)
    YL = device(x, yh, z, 1 - ylo, c)
    ZP = device(x, yh, lax.rem(z + 1, 8), ylo, c)
    ZM = device(x, yh, lax.rem(z + 7, 8), ylo, c)
    SIB = device(x, yh, z, ylo, 1 - c)

    barrier = pltpu.get_barrier_semaphore()
    for dev in (XP, XM, Y, YL, SIB):
        pl.semaphore_signal(barrier, inc=1, device_id=dev, device_id_type=MESH)

    @pl.when(c == 0)
    def _():
        for dev in (ZP, ZM):
            pl.semaphore_signal(barrier, inc=1, device_id=dev, device_id_type=MESH)

    def columns(r, core):
        chip = (yh if r < 4 else 1 - yh) * 4 + lax.rem(x + r % 4, 4)
        return pl.ds(pl.multiple_of(chip * 512 + core * 256, 256), 256)

    def lanes(r):
        return pl.ds(r * 256, 256)

    locals_ = []

    def load(src, dst):
        cp = pltpu.make_async_copy(src, dst, lsem.at[len(locals_)])
        cp.start()
        locals_.append(cp)
        return cp

    load_x = [load(x_hbm.at[:, columns(r, c)], Xb.at[0, :, lanes(r)]) for r in range(8)]
    load_c = load(c_hbm, Cb.at[0])
    load_w = load(w_hbm.at[0], Wb.at[0])
    load_ps = []
    for dz in (4, 3, 5, 2, 6, 1, 7, 0):
        for b in range(2):
            cols = pl.ds(pl.multiple_of(b * HALF + lax.rem(z + dz, 8) * FC, FC), FC)
            load_ps.append(load(ps_hbm.at[0, :, cols], PSb.at[dz, b]))
    load_o = [load(op_hbm, OPb), load(om_hbm, OMb)]

    sent = {}

    def send(name, src, dst, dev):
        i = NUMBER[name]
        cp = pltpu.make_async_remote_copy(
            src_ref=src, dst_ref=dst, send_sem=ssem.at[i], recv_sem=rsem.at[i],
            device_id=dev, device_id_type=MESH,
        )
        cp.start()
        sent[name] = cp

    here = set()

    def arrived(*names):
        for name in names:
            if name not in here:
                here.add(name)
                sent[name].wait_recv()

    def rows_loop(n, body):
        @pl.loop(0, n // 16)
        def _(i):
            body(lambda base: pl.ds(pl.multiple_of(base + i * 16, 16), 16))

    contract = (((0,), (0,)), ((), ()))

    def own_term(r):
        @pl.loop(0, 2)
        def _(j):
            cols = pl.ds(pl.multiple_of(j * 512, 512), 512)
            TO[r, :, cols] = lax.dot_general(
                Xb[0, :, lanes(r)], Cb[0, :, cols], contract, preferred_element_type=f32
            ).astype(bf16)

    def both_terms(r):
        arrived("cs", "xs%d" % r)

        @pl.loop(0, 2)
        def _(j):
            cols = pl.ds(pl.multiple_of(j * 512, 512), 512)
            other = lax.dot_general(
                Xb[1, :, lanes(r)], Cb[1, :, cols], contract, preferred_element_type=f32
            ).astype(bf16)
            total = TO[r, :, cols].astype(f32) + other.astype(f32)
            T[r, :, cols] = total
            SB[r, :, cols] = total.astype(bf16)

    load_c.wait()
    for cp in load_x:
        cp.wait()
    own_term(rel(2, 0))
    own_term(rel(2, 1))

    @pl.when(c == 0)
    def _():
        pl.semaphore_wait(barrier, 7)
        for i, dev in enumerate((ZP, ZM)):
            pl.semaphore_signal(zsem.at[i], inc=1, device_id=dev, device_id_type=MESH)

    @pl.when(c == 1)
    def _():
        pl.semaphore_wait(barrier, 5)

    send("xpP2", w_hbm.at[0, CUT:ROWS], Wb.at[rel(3, 0), CUT:ROWS], XP)
    send("xmP2", w_hbm.at[0, CUT:ROWS], Wb.at[rel(1, 0), CUT:ROWS], XM)
    send("yP1", w_hbm.at[0, 0:CUT], Wb.at[rel(0, 1), 0:CUT], Y)
    send("cs", c_hbm, Cb.at[1], SIB)
    for r in (rel(2, 0), rel(2, 1), rel(1, 1), rel(3, 1), rel(1, 0), rel(3, 0), rel(0, 1), rel(0, 0)):
        send("xs%d" % r, x_hbm.at[:, columns(r, 1 - c)], Xb.at[1, :, lanes(r)], SIB)
    send("xpP1", w_hbm.at[0, 0:CUT], Wb.at[rel(3, 0), 0:CUT], XP)
    send("xmP1", w_hbm.at[0, 0:CUT], Wb.at[rel(1, 0), 0:CUT], XM)
    send("yP2_0", w_hbm.at[0, CUT:ROWS], Wb.at[rel(0, 1), CUT:ROWS], Y)

    def z_start():
        for cp in load_ps:
            cp.wait()

        @pl.when(c == 0)
        def _():
            for i in range(2):
                pl.semaphore_wait(zsem.at[i], 1)
            pl.semaphore_signal(zsem.at[2], inc=1, device_id=SIB, device_id_type=MESH)

        @pl.when(c == 1)
        def _():
            pl.semaphore_wait(zsem.at[2], 1)

        send("zpL4", PSb.at[4, 0], zraw.at[0, 0], ZP)
        send("zmL4", PSb.at[4, 1], zraw.at[0, 1], ZM)
        send("zpS3", PSb.at[3, 1], zraw.at[1, 0], ZP)
        send("zmS3", PSb.at[5, 0], zraw.at[1, 1], ZM)

    STAGES = ("L3", "S2", "L2", "S1", "L1")

    def ring(stage, before, terms):
        arrived("zp" + before, "zm" + before)
        k = STAGES.index(stage)

        def body(at):
            s = at(0)
            for way, (dz, b) in enumerate(terms):
                if before in STAGES:
                    come = zin[STAGES.index(before), way, s]
                else:
                    come = zraw[("L4", "S3").index(before), way, s].astype(f32)
                zout[k, way, s] = PSb[dz, b, s].astype(f32) + come

        rows_loop(FR, body)
        send("zp" + stage, zout.at[k, 0], zin.at[k, 0], ZP)
        send("zm" + stage, zout.at[k, 1], zin.at[k, 1], ZM)

    def z_total():
        arrived("zpS1", "zmS1", "zpL1", "zmL1")

        def body(at):
            s = at(0)
            ZS[0, s] = PSb[0, 0, s].astype(f32) + zin[4, 0, s] + zin[3, 1, s]
            ZS[1, s] = PSb[0, 1, s].astype(f32) + zin[3, 0, s] + zin[4, 1, s]

        rows_loop(FR, body)
        send("yo", ZS.at[1 - ylo], yr, YL)

    def outer_step():
        for cp in load_o:
            cp.wait()
        arrived("yo")

        def body(at):
            s = at(0)
            average = (ZS[ylo, s] + yr[s]) * (1.0 / 16)
            moment = outer_beta * OMb[s] + average
            params = OPb[s] - outer_rate * (outer_beta * moment + average)
            NM[s] = moment
            NP[s] = params
            LW[0, ylo, s] = params.astype(bf16)

        rows_loop(FR, body)
        send("yl", LW.at[0, ylo], LW.at[0, ylo], YL)
        share("o", 1)

    def share(which, n):
        b = ylo if which == "o" else 1 - ylo
        if n > 1:
            arrived("gp%s%d" % (which, n - 1), "gm%s%d" % (which, n - 1))
        elif which == "q":
            arrived("yl")
        up, down = (9 - n) % 8, n - 1
        if n < 4 or which == "o":
            send("gp%s%d" % (which, n), LW.at[up, b], LW.at[(up + 7) % 8, b], ZP)
        if n < 4 or which == "q":
            send("gm%s%d" % (which, n), LW.at[down, b], LW.at[(down + 1) % 8, b], ZM)

    def a_p2():
        arrived("xpP2", "xmP2")
        send("xpfP2", Wb.at[rel(3, 0), CUT:MID2], Wb.at[rel(2, 0), CUT:MID2], XP)
        send("xmfP2", Wb.at[rel(1, 0), MID2:ROWS], Wb.at[rel(2, 0), MID2:ROWS], XM)
        send("yP2_3", Wb.at[rel(3, 0), CUT:ROWS], Wb.at[rel(3, 1), CUT:ROWS], Y)
        send("yP2_1", Wb.at[rel(1, 0), CUT:ROWS], Wb.at[rel(1, 1), CUT:ROWS], Y)

    def a_q1():
        arrived("yP1")
        send("xpQ1", Wb.at[rel(0, 1), 0:CUT], Wb.at[rel(3, 1), 0:CUT], XP)
        send("xmQ1", Wb.at[rel(0, 1), 0:CUT], Wb.at[rel(1, 1), 0:CUT], XM)

    def a_p1():
        arrived("xpP1", "xmP1")
        send("xpfP1", Wb.at[rel(3, 0), 0:MID1], Wb.at[rel(2, 0), 0:MID1], XP)
        send("xmfP1", Wb.at[rel(1, 0), MID1:CUT], Wb.at[rel(2, 0), MID1:CUT], XM)

    def a_p2far():
        arrived("xpfP2", "xmfP2")
        send("yP2_2a", Wb.at[rel(2, 0), CUT:MID2], Wb.at[rel(2, 1), CUT:MID2], Y)
        send("yP2_2b", Wb.at[rel(2, 0), MID2:ROWS], Wb.at[rel(2, 1), MID2:ROWS], Y)

    def a_fq1():
        arrived("xpQ1", "xmQ1")
        send("xpfQ1", Wb.at[rel(3, 1), 0:MID1], Wb.at[rel(2, 1), 0:MID1], XP)
        send("xmfQ1", Wb.at[rel(1, 1), MID1:CUT], Wb.at[rel(2, 1), MID1:CUT], XM)

    def b_send(dy):
        r = rel(2, dy)
        send("bp%d" % dy, SB.at[r, 0:MID1], rap.at[dy], XP)
        send("bm%d" % dy, SB.at[r, MID1:CUT], ram.at[dy], XM)

    def d_send(dx):
        send("d%d" % dx, SB.at[rel(dx, 1), CUT:ROWS], rd.at[dx], Y)

    def c_plain(dx, dy):
        if dx == 1:
            send("cp%db" % dy, SB.at[rel(1, dy), MID1:CUT], rbp.at[dy, MID1:CUT], XP)
        else:
            send("cm%db" % dy, SB.at[rel(3, dy), 0:MID1], rbm.at[dy, 0:MID1], XM)

    def c_added(dy):
        arrived("bp%d" % dy, "bm%d" % dy)

        def body(at):
            s, t = at(0), at(MID1)
            SB[rel(1, dy), s] = (T[rel(1, dy), s] + rap[dy, s].astype(f32)).astype(bf16)
            SB[rel(3, dy), t] = (T[rel(3, dy), t] + ram[dy, s].astype(f32)).astype(bf16)

        rows_loop(MID1, body)
        send("cp%da" % dy, SB.at[rel(1, dy), 0:MID1], rbp.at[dy, 0:MID1], XP)
        send("cm%da" % dy, SB.at[rel(3, dy), MID1:CUT], rbm.at[dy, MID1:CUT], XM)

    def e_send():
        arrived("cp1a", "cp1b", "cm1a", "cm1b")

        def body(at):
            s = at(0)
            total = T[rel(0, 1), s] + rbp[1, s].astype(f32) + rbm[1, s].astype(f32)
            SB[rel(0, 1), s] = total.astype(bf16)

        rows_loop(CUT, body)
        send("e", SB.at[rel(0, 1), 0:CUT], re, Y)

    def g_send():
        arrived("d2")

        def body(at):
            s, t = at(0), at(CUT)
            SB[rel(2, 0), t] = (T[rel(2, 0), t] + rd[2, s].astype(f32)).astype(bf16)

        rows_loop(ROWS - CUT, body)
        send("gp", SB.at[rel(2, 0), CUT:MID2], rgp, XP)
        send("gm", SB.at[rel(2, 0), MID2:ROWS], rgm, XM)

    def h_send():
        arrived("d1", "d3", "gp", "gm")
        half = MID2 - CUT

        def body(at):
            s, u, t, v = at(0), at(half), at(CUT), at(MID2)
            SB[rel(1, 0), t] = (T[rel(1, 0), t] + rd[1, s].astype(f32) + rgp[s].astype(f32)).astype(bf16)
            SB[rel(1, 0), v] = (T[rel(1, 0), v] + rd[1, u].astype(f32)).astype(bf16)
            SB[rel(3, 0), t] = (T[rel(3, 0), t] + rd[3, s].astype(f32)).astype(bf16)
            SB[rel(3, 0), v] = (T[rel(3, 0), v] + rd[3, u].astype(f32) + rgm[s].astype(f32)).astype(bf16)

        rows_loop(half, body)
        send("hp", SB.at[rel(1, 0), CUT:ROWS], rhp, XP)
        send("hm", SB.at[rel(3, 0), CUT:ROWS], rhm, XM)

    def finish_high():
        arrived("d0", "hp", "hm")

        def body(at):
            s, t = at(0), at(CUT)
            G[t] = T[rel(0, 0), t] + rd[0, s].astype(f32) + rhp[s].astype(f32) + rhm[s].astype(f32)

        rows_loop(ROWS - CUT, body)

    def finish_low():
        arrived("cp0a", "cp0b", "cm0a", "cm0b")

        def body(at):
            s = at(0)
            G[s] = T[rel(0, 0), s] + rbp[0, s].astype(f32) + rbm[0, s].astype(f32)

        rows_loop(CUT, body)
        arrived("e")

        def body2(at):
            s = at(0)
            G[s] = G[s] + re[s].astype(f32)

        rows_loop(CUT, body2)

    def kv_half(slot, h):
        kv_wait()
        dst = KVs if slot == 1 else KVo

        @pl.loop(0, 2)
        def _(j):
            cols = pl.ds(pl.multiple_of(h * 512 + j * 256, 256), 256)
            weights = Wb[:, :, cols].reshape(HALF, 256)
            dst[:, cols] = jnp.dot(Xb[slot], weights, preferred_element_type=f32)

        if slot == 1:
            cols = slice(h * 512, h * 512 + 512)
            send("kv%d" % h, KVs.at[:, cols], KVr.at[:, cols], SIB)

    def kv_wait():
        if "w" not in here:
            here.add("w")
            load_w.wait()
        arrived("yP2_0", "yP2_1", "yP2_3", "yP2_2a", "yP2_2b", "xpfP1", "xmfP1", "xpfQ1", "xmfQ1")

    def kv_finish():
        arrived("kv0", "kv1")

        def body(at):
            s = at(0)
            KVb[s] = (KVo[s] + KVr[s]).astype(bf16)

        rows_loop(TOK, body)

    z_start()
    own_term(4)
    own_term(7)
    both_terms(6)
    ring("L3", "L4", ((3, 0), (5, 1)))
    own_term(5)
    a_p2()
    ring("S2", "S3", ((2, 1), (6, 0)))
    both_terms(2)
    both_terms(5)
    b_send(1)
    both_terms(7)
    ring("L2", "L3", ((2, 0), (6, 1)))
    a_q1()
    own_term(1)
    ring("S1", "S2", ((1, 1), (7, 0)))
    ring("L1", "L2", ((1, 0), (7, 1)))
    c_plain(1, 1)
    c_plain(3, 1)
    a_p1()
    b_send(0)
    d_send(2)
    z_total()
    own_term(0)
    c_added(1)
    both_terms(1)
    a_fq1()
    d_send(1)
    both_terms(4)
    outer_step()
    own_term(3)
    a_p2far()
    g_send()
    share("q", 1)
    d_send(3)
    share("o", 2)
    both_terms(3)
    e_send()
    share("q", 2)
    both_terms(0)
    c_added(0)
    c_plain(1, 0)
    c_plain(3, 0)
    share("o", 3)
    kv_half(0, 0)
    kv_half(1, 0)
    d_send(0)
    h_send()
    share("q", 3)
    share("o", 4)
    kv_half(1, 1)
    share("q", 4)
    kv_half(0, 1)
    finish_low()
    kv_finish()
    finish_high()
    arrived("gpo4", "gmq4")

    for cp in sent.values():
        cp.wait_send()


def write_out(kv, grad, params, moment, weights, kv_out, grad_out, np_out, nm_out, lw_out, sem):
    z = lax.rem(lax.axis_index("replica"), 8)
    pairs = [(kv, kv_out), (grad, grad_out.at[0]), (params, np_out), (moment, nm_out)]
    for dz in range(8):
        for b in range(2):
            cols = pl.ds(pl.multiple_of(b * HALF + lax.rem(z + dz, 8) * FC, FC), FC)
            pairs.append((weights.at[dz, b], lw_out.at[:, cols]))
    copies = [pltpu.make_async_copy(src, dst, sem.at[i]) for i, (src, dst) in enumerate(pairs)]
    for cp in copies:
        cp.start()
    for cp in copies:
        cp.wait()


def on_device(inputs, projection, cotangent, pseudo_grad, outer_params, outer_momentum):
    any_ = pl.BlockSpec(memory_space=pl.ANY)
    inside = pl.BlockSpec(memory_space=pltpu.VMEM)
    vm = pltpu.VMEM
    scratch = [
        vm((2, TOK, HALF), bf16),
        vm((2, TOK, KV), bf16),
        vm((8, ROWS, KV), bf16),
        vm((8, ROWS, KV), bf16),
        vm((8, ROWS, KV), f32),
        vm((8, ROWS, KV), bf16),
        vm((TOK, KV), f32),
        vm((TOK, KV), f32),
        vm((TOK, KV), f32),
        vm((2, MID1, KV), bf16),
        vm((2, MID1, KV), bf16),
        vm((4, ROWS - CUT, KV), bf16),
        vm((2, CUT, KV), bf16),
        vm((2, CUT, KV), bf16),
        vm((CUT, KV), bf16),
        vm((MID2 - CUT, KV), bf16),
        vm((MID2 - CUT, KV), bf16),
        vm((ROWS - CUT, KV), bf16),
        vm((ROWS - CUT, KV), bf16),
        vm((8, 2, FR, FC), bf16),
        vm((2, 2, FR, FC), bf16),
        vm((5, 2, FR, FC), f32),
        vm((5, 2, FR, FC), f32),
        vm((2, FR, FC), f32),
        vm((FR, FC), f32),
        vm((FR, FC), f32),
        vm((FR, FC), f32),
        pltpu.SemaphoreType.DMA((len(MESSAGES),)),
        pltpu.SemaphoreType.DMA((len(MESSAGES),)),
        pltpu.SemaphoreType.DMA((32,)),
        pltpu.SemaphoreType.REGULAR((3,)),
    ]
    operands = (inputs, projection, cotangent, pseudo_grad, outer_params, outer_momentum)
    operands = [pltpu.with_memory_space_constraint(a, pltpu.HBM) for a in operands]
    results = pl.pallas_call(
        kernel,
        out_shape=(
            vm((TOK, KV), bf16),
            vm((ROWS, KV), f32),
            vm((FR, FC), f32),
            vm((FR, FC), f32),
            vm((8, 2, FR, FC), bf16),
        ),
        in_specs=[any_] * 6,
        out_specs=(inside,) * 5,
        scratch_shapes=scratch,
        compiler_params=pltpu.CompilerParams(
            collective_id=0, has_side_effects=True, vmem_limit_bytes=44 * 2**20
        ),
        cost_estimate=pl.CostEstimate(flops=6 * 10**9, bytes_accessed=3 * 10**7, transcendentals=0),
    )(*operands)
    results = [pltpu.with_memory_space_constraint(a, pltpu.VMEM) for a in results]
    return pl.pallas_call(
        write_out,
        out_shape=(
            jax.ShapeDtypeStruct((TOK, KV), bf16),
            jax.ShapeDtypeStruct((1, ROWS, KV), f32),
            jax.ShapeDtypeStruct((FR, FC), f32),
            jax.ShapeDtypeStruct((FR, FC), f32),
            jax.ShapeDtypeStruct((FR, D), bf16),
        ),
        in_specs=[inside] * 5,
        out_specs=(any_,) * 5,
        scratch_shapes=[pltpu.SemaphoreType.DMA((20,))],
        compiler_params=pltpu.CompilerParams(vmem_limit_bytes=44 * 2**20),
    )(*results)


def solution(mesh):
    return jax.shard_map(
        on_device,
        mesh=mesh,
        in_specs=(
            P(("replica", "fsdp"), None),
            P("replica", "fsdp", None),
            P(("replica", "fsdp"), None),
            P("replica", "fsdp", None),
            P("fsdp", "replica"),
            P("fsdp", "replica"),
        ),
        out_specs=(
            P(("replica", "fsdp"), None),
            P("replica", "fsdp", None),
            P("fsdp", "replica"),
            P("fsdp", "replica"),
            P("fsdp", None),
        ),
        check_vma=False,
    )
```

```python
import jax
import jax.numpy as jnp
from jax import lax
from jax.experimental import pallas as pl
from jax.experimental.pallas import tpu as pltpu
from jax.sharding import PartitionSpec as P

outer_rate = 0.7
outer_beta = 0.9

MESH = pl.DeviceIdType.MESH
bf16 = jnp.bfloat16
f32 = jnp.float32

TOK = 384
D = 4096
HALF = 2048
KV = 1024
ROWS = 256
CUT = 160
MID1 = CUT // 2
MID2 = CUT + (ROWS - CUT) // 2
FR = 128
FC = 256

MESSAGES = (
    ["yP1", "yP2_0", "yP2_1", "yP2_3", "yP2_2a", "yP2_2b"]
    + [d + k for d in ("xp", "xm") for k in ("P2", "P1", "Q1", "fP2", "fP1", "fQ1")]
    + ["xs%d" % r for r in range(8)]
    + ["cs", "kv0", "kv1"]
    + ["b%s%d" % (d, y) for d in "pm" for y in (0, 1)]
    + ["c%s%d%s" % (d, y, h) for d in "pm" for y in (0, 1) for h in "ab"]
    + ["d%d" % x for x in range(4)]
    + ["e", "gp", "gm", "hpa", "hpb", "hma", "hmb"]
    + ["z%s%s" % (d, k) for d in "pm" for k in ("L4", "S3", "L3", "S2", "L2", "S1", "L1")]
    + ["yo", "yl"]
    + ["g%s%s%d" % (d, k, n) for d in "pm" for k in "oq" for n in (1, 2, 3)]
    + ["gpo4", "gmq4"]
)
NUMBER = {name: i for i, name in enumerate(MESSAGES)}


def rel(dx, dy):
    return (dx % 4) + 4 * dy


def kernel(
    x_hbm, w_hbm, c_hbm, ps_hbm, op_hbm, om_hbm,
    KVb, G, NP, NM, LW,
    Xb, Cb, Wb, TO, T, SB, KVs, KVo, KVr,
    rap, ram, rd, rbp, rbm, re, rgp, rgm, rhp, rhm,
    PSb, zraw, zout, zin, ZS, yr, OPb, OMb,
    ssem, rsem, lsem, ready,
):
    r_id = lax.axis_index("replica")
    f_id = lax.axis_index("fsdp")
    z = lax.rem(r_id, 8)
    ylo = r_id // 8
    c = lax.rem(f_id, 2)
    x = lax.rem(f_id // 2, 4)
    yh = f_id // 8

    def device(x, yh, z, ylo, c):
        return (ylo * 8 + z, yh * 8 + x * 2 + c)

    XP = device(lax.rem(x + 1, 4), yh, z, ylo, c)
    XM = device(lax.rem(x + 3, 4), yh, z, ylo, c)
    Y = device(x, 1 - yh, z, ylo, c)
    YL = device(x, yh, z, 1 - ylo, c)
    ZP = device(x, yh, lax.rem(z + 1, 8), ylo, c)
    ZM = device(x, yh, lax.rem(z + 7, 8), ylo, c)
    SIB = device(x, yh, z, ylo, 1 - c)

    barrier = pltpu.get_barrier_semaphore()
    NEAR = ("xp", "xm", "y", "yl", "zp", "zm", "sib")
    device_of = dict(xp=XP, xm=XM, y=Y, yl=YL, zp=ZP, zm=ZM, sib=SIB)
    first = dict(xp=x < 3, xm=x == 0, y=yh == 0, yl=ylo == 0, zp=z < 7, zm=z == 0, sib=c == 1)
    back = dict(xp="xm", xm="xp", y="y", yl="yl", zp="zm", zm="zp", sib="sib")

    for k in NEAR:
        @pl.when(first[k])
        def _():
            pl.semaphore_signal(barrier, inc=1, device_id=device_of[k], device_id_type=MESH)

    def gate(k):
        @pl.when(first[k])
        def _():
            pl.semaphore_wait(ready.at[NEAR.index(k)], 1)

    def columns(r, core):
        chip = (yh if r < 4 else 1 - yh) * 4 + lax.rem(x + r % 4, 4)
        return pl.ds(pl.multiple_of(chip * 512 + core * 256, 256), 256)

    def lanes(r):
        return pl.ds(r * 256, 256)

    locals_ = []

    def load(src, dst):
        cp = pltpu.make_async_copy(src, dst, lsem.at[len(locals_)])
        cp.start()
        locals_.append(cp)
        return cp

    load_x = [load(x_hbm.at[:, columns(r, c)], Xb.at[0, :, lanes(r)]) for r in range(8)]
    load_c = load(c_hbm, Cb.at[0])
    load_w = load(w_hbm.at[0], Wb.at[0])
    load_ps = []
    for dz in (4, 3, 5, 2, 6, 1, 7, 0):
        for b in range(2):
            cols = pl.ds(pl.multiple_of(b * HALF + lax.rem(z + dz, 8) * FC, FC), FC)
            load_ps.append(load(ps_hbm.at[0, :, cols], PSb.at[dz, b]))
    load_o = [load(op_hbm, OPb), load(om_hbm, OMb)]

    sent = {}

    def send(name, src, dst, dev):
        i = NUMBER[name]
        cp = pltpu.make_async_remote_copy(
            src_ref=src, dst_ref=dst, send_sem=ssem.at[i], recv_sem=rsem.at[i],
            device_id=dev, device_id_type=MESH,
        )
        cp.start()
        sent[name] = cp

    here = set()

    def arrived(*names):
        for name in names:
            if name not in here:
                here.add(name)
                sent[name].wait_recv()

    def rows_loop(n, body):
        @pl.loop(0, n // 16)
        def _(i):
            body(lambda base: pl.ds(pl.multiple_of(base + i * 16, 16), 16))

    contract = (((0,), (0,)), ((), ()))

    def own_term(r):
        @pl.loop(0, 2)
        def _(j):
            cols = pl.ds(pl.multiple_of(j * 512, 512), 512)
            TO[r, :, cols] = lax.dot_general(
                Xb[0, :, lanes(r)], Cb[0, :, cols], contract, preferred_element_type=f32
            ).astype(bf16)

    def both_terms(r):
        arrived("cs", "xs%d" % r)

        @pl.loop(0, 2)
        def _(j):
            cols = pl.ds(pl.multiple_of(j * 512, 512), 512)
            other = lax.dot_general(
                Xb[1, :, lanes(r)], Cb[1, :, cols], contract, preferred_element_type=f32
            ).astype(bf16)
            total = TO[r, :, cols].astype(f32) + other.astype(f32)
            T[r, :, cols] = total
            SB[r, :, cols] = total.astype(bf16)

    greeted = sum(jnp.where(first[k], 0, 1) for k in NEAR)

    @pl.when(greeted > 0)
    def _():
        pl.semaphore_wait(barrier, greeted)

    for k in NEAR:
        @pl.when(jnp.logical_not(first[k]))
        def _():
            pl.semaphore_signal(
                ready.at[NEAR.index(back[k])], inc=1, device_id=device_of[k], device_id_type=MESH
            )

    gate("xp")
    send("xpP2", w_hbm.at[0, CUT:ROWS], Wb.at[rel(3, 0), CUT:ROWS], XP)
    send("xpP1", w_hbm.at[0, 0:CUT], Wb.at[rel(3, 0), 0:CUT], XP)
    gate("xm")
    send("xmP2", w_hbm.at[0, CUT:ROWS], Wb.at[rel(1, 0), CUT:ROWS], XM)
    send("xmP1", w_hbm.at[0, 0:CUT], Wb.at[rel(1, 0), 0:CUT], XM)
    gate("y")
    send("yP1", w_hbm.at[0, 0:CUT], Wb.at[rel(0, 1), 0:CUT], Y)
    send("yP2_0", w_hbm.at[0, CUT:ROWS], Wb.at[rel(0, 1), CUT:ROWS], Y)
    gate("sib")
    send("cs", c_hbm, Cb.at[1], SIB)
    for r in (rel(2, 0), rel(2, 1), rel(1, 1), rel(3, 1), rel(1, 0), rel(3, 0), rel(0, 1), rel(0, 0)):
        send("xs%d" % r, x_hbm.at[:, columns(r, 1 - c)], Xb.at[1, :, lanes(r)], SIB)

    load_c.wait()
    for cp in load_x:
        cp.wait()
    own_term(rel(2, 0))
    own_term(rel(2, 1))

    def z_start():
        for cp in load_ps:
            cp.wait()

        gate("zp")
        send("zpL4", PSb.at[4, 0], zraw.at[0, 0], ZP)
        send("zpS3", PSb.at[3, 1], zraw.at[1, 0], ZP)
        gate("zm")
        send("zmL4", PSb.at[4, 1], zraw.at[0, 1], ZM)
        send("zmS3", PSb.at[5, 0], zraw.at[1, 1], ZM)

    STAGES = ("L3", "S2", "L2", "S1", "L1")

    def ring(stage, before, terms):
        arrived("zp" + before, "zm" + before)
        k = STAGES.index(stage)

        def body(at):
            s = at(0)
            for way, (dz, b) in enumerate(terms):
                if before in STAGES:
                    come = zin[STAGES.index(before), way, s]
                else:
                    come = zraw[("L4", "S3").index(before), way, s].astype(f32)
                zout[k, way, s] = PSb[dz, b, s].astype(f32) + come

        rows_loop(FR, body)
        send("zp" + stage, zout.at[k, 0], zin.at[k, 0], ZP)
        send("zm" + stage, zout.at[k, 1], zin.at[k, 1], ZM)

    def z_total():
        arrived("zpS1", "zmS1", "zpL1", "zmL1")

        def body(at):
            s = at(0)
            ZS[0, s] = PSb[0, 0, s].astype(f32) + zin[4, 0, s] + zin[3, 1, s]
            ZS[1, s] = PSb[0, 1, s].astype(f32) + zin[3, 0, s] + zin[4, 1, s]

        rows_loop(FR, body)
        gate("yl")
        send("yo", ZS.at[1 - ylo], yr, YL)

    def outer_step():
        for cp in load_o:
            cp.wait()
        arrived("yo")

        def body(at):
            s = at(0)
            average = (ZS[ylo, s] + yr[s]) * (1.0 / 16)
            moment = outer_beta * OMb[s] + average
            params = OPb[s] - outer_rate * (outer_beta * moment + average)
            NM[s] = moment
            NP[s] = params
            LW[0, ylo, s] = params.astype(bf16)

        rows_loop(FR, body)
        send("yl", LW.at[0, ylo], LW.at[0, ylo], YL)
        share("o", 1)

    def share(which, n):
        b = ylo if which == "o" else 1 - ylo
        if n > 1:
            arrived("gp%s%d" % (which, n - 1), "gm%s%d" % (which, n - 1))
        elif which == "q":
            arrived("yl")
        up, down = (9 - n) % 8, n - 1
        if n < 4 or which == "o":
            send("gp%s%d" % (which, n), LW.at[up, b], LW.at[(up + 7) % 8, b], ZP)
        if n < 4 or which == "q":
            send("gm%s%d" % (which, n), LW.at[down, b], LW.at[(down + 1) % 8, b], ZM)

    def a_p2():
        arrived("xpP2", "xmP2")
        send("xpfP2", Wb.at[rel(3, 0), CUT:MID2], Wb.at[rel(2, 0), CUT:MID2], XP)
        send("xmfP2", Wb.at[rel(1, 0), MID2:ROWS], Wb.at[rel(2, 0), MID2:ROWS], XM)
        send("yP2_3", Wb.at[rel(3, 0), CUT:ROWS], Wb.at[rel(3, 1), CUT:ROWS], Y)
        send("yP2_1", Wb.at[rel(1, 0), CUT:ROWS], Wb.at[rel(1, 1), CUT:ROWS], Y)

    def a_q1():
        arrived("yP1")
        send("xpQ1", Wb.at[rel(0, 1), 0:CUT], Wb.at[rel(3, 1), 0:CUT], XP)
        send("xmQ1", Wb.at[rel(0, 1), 0:CUT], Wb.at[rel(1, 1), 0:CUT], XM)

    def a_p1():
        arrived("xpP1", "xmP1")
        send("xpfP1", Wb.at[rel(3, 0), 0:MID1], Wb.at[rel(2, 0), 0:MID1], XP)
        send("xmfP1", Wb.at[rel(1, 0), MID1:CUT], Wb.at[rel(2, 0), MID1:CUT], XM)

    def a_p2far():
        arrived("xpfP2", "xmfP2")
        send("yP2_2a", Wb.at[rel(2, 0), CUT:MID2], Wb.at[rel(2, 1), CUT:MID2], Y)
        send("yP2_2b", Wb.at[rel(2, 0), MID2:ROWS], Wb.at[rel(2, 1), MID2:ROWS], Y)

    def a_fq1():
        arrived("xpQ1", "xmQ1")
        send("xpfQ1", Wb.at[rel(3, 1), 0:MID1], Wb.at[rel(2, 1), 0:MID1], XP)
        send("xmfQ1", Wb.at[rel(1, 1), MID1:CUT], Wb.at[rel(2, 1), MID1:CUT], XM)

    def b_send(dy):
        r = rel(2, dy)
        send("bp%d" % dy, SB.at[r, 0:MID1], rap.at[dy], XP)
        send("bm%d" % dy, SB.at[r, MID1:CUT], ram.at[dy], XM)

    def d_send(dx):
        send("d%d" % dx, SB.at[rel(dx, 1), CUT:ROWS], rd.at[dx], Y)

    def c_plain(dx, dy):
        if dx == 1:
            send("cp%db" % dy, SB.at[rel(1, dy), MID1:CUT], rbp.at[dy, MID1:CUT], XP)
        else:
            send("cm%db" % dy, SB.at[rel(3, dy), 0:MID1], rbm.at[dy, 0:MID1], XM)

    def c_added(dy):
        arrived("bp%d" % dy, "bm%d" % dy)

        def body(at):
            s, t = at(0), at(MID1)
            SB[rel(1, dy), s] = (T[rel(1, dy), s] + rap[dy, s].astype(f32)).astype(bf16)
            SB[rel(3, dy), t] = (T[rel(3, dy), t] + ram[dy, s].astype(f32)).astype(bf16)

        rows_loop(MID1, body)
        send("cp%da" % dy, SB.at[rel(1, dy), 0:MID1], rbp.at[dy, 0:MID1], XP)
        send("cm%da" % dy, SB.at[rel(3, dy), MID1:CUT], rbm.at[dy, MID1:CUT], XM)

    def e_send():
        arrived("cp1a", "cp1b", "cm1a", "cm1b")

        def body(at):
            s = at(0)
            total = T[rel(0, 1), s] + rbp[1, s].astype(f32) + rbm[1, s].astype(f32)
            SB[rel(0, 1), s] = total.astype(bf16)

        rows_loop(CUT, body)
        send("e", SB.at[rel(0, 1), 0:CUT], re, Y)

    def g_send():
        arrived("d2")

        def body(at):
            s, t = at(0), at(CUT)
            SB[rel(2, 0), t] = (T[rel(2, 0), t] + rd[2, s].astype(f32)).astype(bf16)

        rows_loop(ROWS - CUT, body)
        send("gp", SB.at[rel(2, 0), CUT:MID2], rgp, XP)
        send("gm", SB.at[rel(2, 0), MID2:ROWS], rgm, XM)

    def h_send():
        arrived("d1", "d3", "gp", "gm")
        half = MID2 - CUT

        def body(at):
            s, u, t, v = at(0), at(half), at(CUT), at(MID2)
            SB[rel(1, 0), t] = (T[rel(1, 0), t] + rd[1, s].astype(f32) + rgp[s].astype(f32)).astype(bf16)
            SB[rel(1, 0), v] = (T[rel(1, 0), v] + rd[1, u].astype(f32)).astype(bf16)
            SB[rel(3, 0), t] = (T[rel(3, 0), t] + rd[3, s].astype(f32)).astype(bf16)
            SB[rel(3, 0), v] = (T[rel(3, 0), v] + rd[3, u].astype(f32) + rgm[s].astype(f32)).astype(bf16)

        rows_loop(half, body)
        send("hpa", SB.at[rel(1, 0), CUT:MID2], rhp.at[0:half], XP)
        send("hma", SB.at[rel(3, 0), CUT:MID2], rhm.at[0:half], XM)
        send("hpb", SB.at[rel(1, 0), MID2:ROWS], rhp.at[half : ROWS - CUT], XP)
        send("hmb", SB.at[rel(3, 0), MID2:ROWS], rhm.at[half : ROWS - CUT], XM)

    def finish_high(part):
        arrived("d0", "hp" + part, "hm" + part)
        half = MID2 - CUT
        first = 0 if part == "a" else half

        def body(at):
            s, t = at(first), at(CUT + first)
            G[t] = T[rel(0, 0), t] + rd[0, s].astype(f32) + rhp[s].astype(f32) + rhm[s].astype(f32)

        rows_loop(half, body)

    def finish_low():
        arrived("cp0a", "cp0b", "cm0a", "cm0b")

        def body(at):
            s = at(0)
            G[s] = T[rel(0, 0), s] + rbp[0, s].astype(f32) + rbm[0, s].astype(f32)

        rows_loop(CUT, body)
        arrived("e")

        def body2(at):
            s = at(0)
            G[s] = G[s] + re[s].astype(f32)

        rows_loop(CUT, body2)

    def kv_half(slot, h):
        kv_wait()
        dst = KVs if slot == 1 else KVo

        @pl.loop(0, 2)
        def _(j):
            cols = pl.ds(pl.multiple_of(h * 512 + j * 256, 256), 256)
            weights = Wb[:, :, cols].reshape(HALF, 256)
            dst[:, cols] = jnp.dot(Xb[slot], weights, preferred_element_type=f32)

        if slot == 1:
            cols = slice(h * 512, h * 512 + 512)
            send("kv%d" % h, KVs.at[:, cols], KVr.at[:, cols], SIB)

    def kv_wait():
        if "w" not in here:
            here.add("w")
            load_w.wait()
        arrived("yP2_0", "yP2_1", "yP2_3", "yP2_2a", "yP2_2b", "xpfP1", "xmfP1", "xpfQ1", "xmfQ1")

    def kv_finish():
        arrived("kv0", "kv1")

        def body(at):
            s = at(0)
            KVb[s] = (KVo[s] + KVr[s]).astype(bf16)

        rows_loop(TOK, body)

    done = set()

    def all_sent(*later):
        for name, cp in sent.items():
            if name not in done and not name.startswith(later or ("none",)):
                done.add(name)
                cp.wait_send()

    z_start()
    own_term(4)
    own_term(7)
    both_terms(6)
    ring("L3", "L4", ((3, 0), (5, 1)))
    own_term(5)
    a_p2()
    ring("S2", "S3", ((2, 1), (6, 0)))
    both_terms(2)
    both_terms(5)
    b_send(1)
    both_terms(7)
    ring("L2", "L3", ((2, 0), (6, 1)))
    a_q1()
    own_term(1)
    ring("S1", "S2", ((1, 1), (7, 0)))
    ring("L1", "L2", ((1, 0), (7, 1)))
    c_plain(1, 1)
    c_plain(3, 1)
    a_p1()
    b_send(0)
    d_send(2)
    z_total()
    own_term(0)
    c_added(1)
    both_terms(1)
    a_fq1()
    d_send(1)
    both_terms(4)
    outer_step()
    own_term(3)
    a_p2far()
    g_send()
    share("q", 1)
    d_send(3)
    share("o", 2)
    both_terms(3)
    e_send()
    share("q", 2)
    both_terms(0)
    c_added(0)
    c_plain(1, 0)
    c_plain(3, 0)
    share("o", 3)
    kv_half(0, 0)
    kv_half(1, 0)
    d_send(0)
    h_send()
    share("q", 3)
    share("o", 4)
    kv_half(1, 1)
    share("q", 4)
    kv_half(0, 1)
    all_sent("c", "d0", "e", "h", "gpo4", "gmq4")
    finish_low()
    kv_finish()
    finish_high("a")
    finish_high("b")
    arrived("gpo4", "gmq4")

    all_sent()


def write_out(kv, grad, params, moment, weights, kv_out, grad_out, np_out, nm_out, lw_out, sem):
    z = lax.rem(lax.axis_index("replica"), 8)
    pairs = [(kv, kv_out), (grad, grad_out.at[0]), (params, np_out), (moment, nm_out)]
    for dz in range(8):
        for b in range(2):
            cols = pl.ds(pl.multiple_of(b * HALF + lax.rem(z + dz, 8) * FC, FC), FC)
            pairs.append((weights.at[dz, b], lw_out.at[:, cols]))
    copies = [pltpu.make_async_copy(src, dst, sem.at[i]) for i, (src, dst) in enumerate(pairs)]
    for cp in copies:
        cp.start()
    for cp in copies:
        cp.wait()


def on_device(inputs, projection, cotangent, pseudo_grad, outer_params, outer_momentum):
    any_ = pl.BlockSpec(memory_space=pl.ANY)
    inside = pl.BlockSpec(memory_space=pltpu.VMEM)
    vm = pltpu.VMEM
    scratch = [
        vm((2, TOK, HALF), bf16),
        vm((2, TOK, KV), bf16),
        vm((8, ROWS, KV), bf16),
        vm((8, ROWS, KV), bf16),
        vm((8, ROWS, KV), f32),
        vm((8, ROWS, KV), bf16),
        vm((TOK, KV), f32),
        vm((TOK, KV), f32),
        vm((TOK, KV), f32),
        vm((2, MID1, KV), bf16),
        vm((2, MID1, KV), bf16),
        vm((4, ROWS - CUT, KV), bf16),
        vm((2, CUT, KV), bf16),
        vm((2, CUT, KV), bf16),
        vm((CUT, KV), bf16),
        vm((MID2 - CUT, KV), bf16),
        vm((MID2 - CUT, KV), bf16),
        vm((ROWS - CUT, KV), bf16),
        vm((ROWS - CUT, KV), bf16),
        vm((8, 2, FR, FC), bf16),
        vm((2, 2, FR, FC), bf16),
        vm((5, 2, FR, FC), f32),
        vm((5, 2, FR, FC), f32),
        vm((2, FR, FC), f32),
        vm((FR, FC), f32),
        vm((FR, FC), f32),
        vm((FR, FC), f32),
        pltpu.SemaphoreType.DMA((len(MESSAGES),)),
        pltpu.SemaphoreType.DMA((len(MESSAGES),)),
        pltpu.SemaphoreType.DMA((32,)),
        pltpu.SemaphoreType.REGULAR((7,)),
    ]
    operands = (inputs, projection, cotangent, pseudo_grad, outer_params, outer_momentum)
    operands = [pltpu.with_memory_space_constraint(a, pltpu.HBM) for a in operands]
    results = pl.pallas_call(
        kernel,
        out_shape=(
            vm((TOK, KV), bf16),
            vm((ROWS, KV), f32),
            vm((FR, FC), f32),
            vm((FR, FC), f32),
            vm((8, 2, FR, FC), bf16),
        ),
        in_specs=[any_] * 6,
        out_specs=(inside,) * 5,
        scratch_shapes=scratch,
        compiler_params=pltpu.CompilerParams(
            collective_id=0, has_side_effects=True, vmem_limit_bytes=44 * 2**20
        ),
        cost_estimate=pl.CostEstimate(flops=6 * 10**9, bytes_accessed=3 * 10**7, transcendentals=0),
    )(*operands)
    results = [pltpu.with_memory_space_constraint(a, pltpu.VMEM) for a in results]
    return pl.pallas_call(
        write_out,
        out_shape=(
            jax.ShapeDtypeStruct((TOK, KV), bf16),
            jax.ShapeDtypeStruct((1, ROWS, KV), f32),
            jax.ShapeDtypeStruct((FR, FC), f32),
            jax.ShapeDtypeStruct((FR, FC), f32),
            jax.ShapeDtypeStruct((FR, D), bf16),
        ),
        in_specs=[inside] * 5,
        out_specs=(any_,) * 5,
        scratch_shapes=[pltpu.SemaphoreType.DMA((20,))],
        compiler_params=pltpu.CompilerParams(vmem_limit_bytes=44 * 2**20),
    )(*results)


def solution(mesh):
    return jax.shard_map(
        on_device,
        mesh=mesh,
        in_specs=(
            P(("replica", "fsdp"), None),
            P("replica", "fsdp", None),
            P(("replica", "fsdp"), None),
            P("replica", "fsdp", None),
            P("fsdp", "replica"),
            P("fsdp", "replica"),
        ),
        out_specs=(
            P(("replica", "fsdp"), None),
            P("replica", "fsdp", None),
            P("fsdp", "replica"),
            P("fsdp", "replica"),
            P("fsdp", None),
        ),
        check_vma=False,
    )
```

```python
import jax
import jax.numpy as jnp
from jax import lax
from jax.experimental import pallas as pl
from jax.experimental.pallas import tpu as pltpu
from jax.sharding import PartitionSpec as P

outer_rate = 0.7
outer_beta = 0.9

MESH = pl.DeviceIdType.MESH
bf16 = jnp.bfloat16
f32 = jnp.float32

TOK = 384
D = 4096
HALF = 2048
KV = 1024
ROWS = 256
CUT = 160
MID1 = CUT // 2
MID2 = CUT + (ROWS - CUT) // 2
FR = 128
FC = 256

MESSAGES = (
    ["yP1", "yP2_0", "yP2_1", "yP2_3", "yP2_2a", "yP2_2b"]
    + [d + k for d in ("xp", "xm") for k in ("P2", "P1", "Q1", "fP2", "fP1", "fQ1")]
    + ["xs%d" % r for r in range(8)]
    + ["cs", "kv0", "kv1"]
    + ["b%s%d" % (d, y) for d in "pm" for y in (0, 1)]
    + ["c%s%d%s" % (d, y, h) for d in "pm" for y in (0, 1) for h in "ab"]
    + ["d%d" % x for x in range(4)]
    + ["e", "gp", "gm", "hpa", "hpb", "hma", "hmb"]
    + ["z%s%s" % (d, k) for d in "pm" for k in ("L4", "S3", "L3", "S2", "L2", "S1", "L1")]
    + ["yo", "yl"]
    + ["g%s%s%d" % (d, k, n) for d in "pm" for k in "oq" for n in (1, 2, 3)]
    + ["gpo4", "gmq4"]
)
NUMBER = {name: i for i, name in enumerate(MESSAGES)}


def rel(dx, dy):
    return (dx % 4) + 4 * dy


def kernel(
    x_hbm, w_hbm, c_hbm, ps_hbm, op_hbm, om_hbm,
    KVb, G, NP, NM, LW,
    Xb, Cb, Wb, TO, T, SB, KVs, KVo, KVr,
    rap, ram, rd, rbp, rbm, re, rgp, rgm, rhp, rhm,
    PSb, zraw, zout, zin, ZS, yr, OPb, OMb,
    ssem, rsem, lsem, ready,
):
    r_id = lax.axis_index("replica")
    f_id = lax.axis_index("fsdp")
    z = lax.rem(r_id, 8)
    ylo = r_id // 8
    c = lax.rem(f_id, 2)
    x = lax.rem(f_id // 2, 4)
    yh = f_id // 8

    def device(x, yh, z, ylo, c):
        return (ylo * 8 + z, yh * 8 + x * 2 + c)

    XP = device(lax.rem(x + 1, 4), yh, z, ylo, c)
    XM = device(lax.rem(x + 3, 4), yh, z, ylo, c)
    Y = device(x, 1 - yh, z, ylo, c)
    YL = device(x, yh, z, 1 - ylo, c)
    ZP = device(x, yh, lax.rem(z + 1, 8), ylo, c)
    ZM = device(x, yh, lax.rem(z + 7, 8), ylo, c)
    SIB = device(x, yh, z, ylo, 1 - c)

    barrier = pltpu.get_barrier_semaphore()
    NEAR = ("xp", "xm", "y", "yl", "zp", "zm", "sib")
    device_of = dict(xp=XP, xm=XM, y=Y, yl=YL, zp=ZP, zm=ZM, sib=SIB)
    first = dict(xp=x < 3, xm=x == 0, y=yh == 0, yl=ylo == 0, zp=z < 7, zm=z == 0, sib=c == 0)
    back = dict(xp="xm", xm="xp", y="y", yl="yl", zp="zm", zm="zp", sib="sib")

    for k in NEAR:
        @pl.when(first[k])
        def _():
            pl.semaphore_signal(barrier, inc=1, device_id=device_of[k], device_id_type=MESH)

    def gate(k):
        @pl.when(first[k])
        def _():
            pl.semaphore_wait(ready.at[NEAR.index(k)], 1)

    def columns(r, core):
        chip = (yh if r < 4 else 1 - yh) * 4 + lax.rem(x + r % 4, 4)
        return pl.ds(pl.multiple_of(chip * 512 + core * 256, 256), 256)

    def lanes(r):
        return pl.ds(r * 256, 256)

    locals_ = []

    def load(src, dst):
        cp = pltpu.make_async_copy(src, dst, lsem.at[len(locals_)])
        cp.start()
        locals_.append(cp)
        return cp

    load_x = [load(x_hbm.at[:, columns(r, c)], Xb.at[0, :, lanes(r)]) for r in range(8)]
    load_c = load(c_hbm, Cb.at[0])
    load_w = load(w_hbm.at[0], Wb.at[0])
    load_ps = []
    for dz in (4, 3, 5, 2, 6, 1, 7, 0):
        for b in range(2):
            cols = pl.ds(pl.multiple_of(b * HALF + lax.rem(z + dz, 8) * FC, FC), FC)
            load_ps.append(load(ps_hbm.at[0, :, cols], PSb.at[dz, b]))
    load_o = [load(op_hbm, OPb), load(om_hbm, OMb)]

    sent = {}

    def send(name, src, dst, dev):
        i = NUMBER[name]
        cp = pltpu.make_async_remote_copy(
            src_ref=src, dst_ref=dst, send_sem=ssem.at[i], recv_sem=rsem.at[i],
            device_id=dev, device_id_type=MESH,
        )
        cp.start()
        sent[name] = cp

    here = set()

    def arrived(*names):
        for name in names:
            if name not in here:
                here.add(name)
                sent[name].wait_recv()

    def rows_loop(n, body):
        @pl.loop(0, n // 16)
        def _(i):
            body(lambda base: pl.ds(pl.multiple_of(base + i * 16, 16), 16))

    contract = (((0,), (0,)), ((), ()))

    def own_term(r):
        @pl.loop(0, 2)
        def _(j):
            cols = pl.ds(pl.multiple_of(j * 512, 512), 512)
            TO[r, :, cols] = lax.dot_general(
                Xb[0, :, lanes(r)], Cb[0, :, cols], contract, preferred_element_type=f32
            ).astype(bf16)

    def both_terms(r):
        arrived("cs", "xs%d" % r)

        @pl.loop(0, 2)
        def _(j):
            cols = pl.ds(pl.multiple_of(j * 512, 512), 512)
            other = lax.dot_general(
                Xb[1, :, lanes(r)], Cb[1, :, cols], contract, preferred_element_type=f32
            ).astype(bf16)
            total = TO[r, :, cols].astype(f32) + other.astype(f32)
            T[r, :, cols] = total
            SB[r, :, cols] = total.astype(bf16)

    greeted = sum(jnp.where(first[k], 0, 1) for k in NEAR)

    @pl.when(greeted > 0)
    def _():
        pl.semaphore_wait(barrier, greeted)

    for k in NEAR:
        @pl.when(jnp.logical_not(first[k]))
        def _():
            pl.semaphore_signal(
                ready.at[NEAR.index(back[k])], inc=1, device_id=device_of[k], device_id_type=MESH
            )

    gate("xp")
    send("xpP2", w_hbm.at[0, CUT:ROWS], Wb.at[rel(3, 0), CUT:ROWS], XP)
    send("xpP1", w_hbm.at[0, 0:CUT], Wb.at[rel(3, 0), 0:CUT], XP)
    gate("xm")
    send("xmP2", w_hbm.at[0, CUT:ROWS], Wb.at[rel(1, 0), CUT:ROWS], XM)
    send("xmP1", w_hbm.at[0, 0:CUT], Wb.at[rel(1, 0), 0:CUT], XM)
    gate("y")
    send("yP1", w_hbm.at[0, 0:CUT], Wb.at[rel(0, 1), 0:CUT], Y)
    send("yP2_0", w_hbm.at[0, CUT:ROWS], Wb.at[rel(0, 1), CUT:ROWS], Y)
    gate("sib")
    send("cs", c_hbm, Cb.at[1], SIB)
    for r in (rel(2, 0), rel(2, 1), rel(1, 1), rel(3, 1), rel(1, 0), rel(3, 0), rel(0, 1), rel(0, 0)):
        send("xs%d" % r, x_hbm.at[:, columns(r, 1 - c)], Xb.at[1, :, lanes(r)], SIB)

    load_c.wait()
    for cp in load_x:
        cp.wait()
    own_term(rel(2, 0))
    own_term(rel(2, 1))

    def z_start():
        for cp in load_ps:
            cp.wait()

        gate("zp")
        send("zpL4", PSb.at[4, 0], zraw.at[0, 0], ZP)
        send("zpS3", PSb.at[3, 1], zraw.at[1, 0], ZP)
        gate("zm")
        send("zmL4", PSb.at[4, 1], zraw.at[0, 1], ZM)
        send("zmS3", PSb.at[5, 0], zraw.at[1, 1], ZM)

    STAGES = ("L3", "S2", "L2", "S1", "L1")

    def ring(stage, before, terms):
        arrived("zp" + before, "zm" + before)
        k = STAGES.index(stage)

        def body(at):
            s = at(0)
            for way, (dz, b) in enumerate(terms):
                if before in STAGES:
                    come = zin[STAGES.index(before), way, s]
                else:
                    come = zraw[("L4", "S3").index(before), way, s].astype(f32)
                zout[k, way, s] = PSb[dz, b, s].astype(f32) + come

        rows_loop(FR, body)
        send("zp" + stage, zout.at[k, 0], zin.at[k, 0], ZP)
        send("zm" + stage, zout.at[k, 1], zin.at[k, 1], ZM)

    def z_total():
        arrived("zpS1", "zmS1", "zpL1", "zmL1")

        def body(at):
            s = at(0)
            ZS[0, s] = PSb[0, 0, s].astype(f32) + zin[4, 0, s] + zin[3, 1, s]
            ZS[1, s] = PSb[0, 1, s].astype(f32) + zin[3, 0, s] + zin[4, 1, s]

        rows_loop(FR, body)
        gate("yl")
        send("yo", ZS.at[1 - ylo], yr, YL)

    def outer_step():
        for cp in load_o:
            cp.wait()
        arrived("yo")

        def body(at):
            s = at(0)
            average = (ZS[ylo, s] + yr[s]) * (1.0 / 16)
            moment = outer_beta * OMb[s] + average
            params = OPb[s] - outer_rate * (outer_beta * moment + average)
            NM[s] = moment
            NP[s] = params
            LW[0, ylo, s] = params.astype(bf16)

        rows_loop(FR, body)
        send("yl", LW.at[0, ylo], LW.at[0, ylo], YL)
        share("o", 1)

    def share(which, n):
        b = ylo if which == "o" else 1 - ylo
        if n > 1:
            arrived("gp%s%d" % (which, n - 1), "gm%s%d" % (which, n - 1))
        elif which == "q":
            arrived("yl")
        up, down = (9 - n) % 8, n - 1
        if n < 4 or which == "o":
            send("gp%s%d" % (which, n), LW.at[up, b], LW.at[(up + 7) % 8, b], ZP)
        if n < 4 or which == "q":
            send("gm%s%d" % (which, n), LW.at[down, b], LW.at[(down + 1) % 8, b], ZM)

    def a_p2():
        arrived("xpP2", "xmP2")
        send("xpfP2", Wb.at[rel(3, 0), CUT:MID2], Wb.at[rel(2, 0), CUT:MID2], XP)
        send("xmfP2", Wb.at[rel(1, 0), MID2:ROWS], Wb.at[rel(2, 0), MID2:ROWS], XM)
        send("yP2_3", Wb.at[rel(3, 0), CUT:ROWS], Wb.at[rel(3, 1), CUT:ROWS], Y)
        send("yP2_1", Wb.at[rel(1, 0), CUT:ROWS], Wb.at[rel(1, 1), CUT:ROWS], Y)

    def a_q1():
        arrived("yP1")
        send("xpQ1", Wb.at[rel(0, 1), 0:CUT], Wb.at[rel(3, 1), 0:CUT], XP)
        send("xmQ1", Wb.at[rel(0, 1), 0:CUT], Wb.at[rel(1, 1), 0:CUT], XM)

    def a_p1():
        arrived("xpP1", "xmP1")
        send("xpfP1", Wb.at[rel(3, 0), 0:MID1], Wb.at[rel(2, 0), 0:MID1], XP)
        send("xmfP1", Wb.at[rel(1, 0), MID1:CUT], Wb.at[rel(2, 0), MID1:CUT], XM)

    def a_p2far():
        arrived("xpfP2", "xmfP2")
        send("yP2_2a", Wb.at[rel(2, 0), CUT:MID2], Wb.at[rel(2, 1), CUT:MID2], Y)
        send("yP2_2b", Wb.at[rel(2, 0), MID2:ROWS], Wb.at[rel(2, 1), MID2:ROWS], Y)

    def a_fq1():
        arrived("xpQ1", "xmQ1")
        send("xpfQ1", Wb.at[rel(3, 1), 0:MID1], Wb.at[rel(2, 1), 0:MID1], XP)
        send("xmfQ1", Wb.at[rel(1, 1), MID1:CUT], Wb.at[rel(2, 1), MID1:CUT], XM)

    def b_send(dy):
        r = rel(2, dy)
        send("bp%d" % dy, SB.at[r, 0:MID1], rap.at[dy], XP)
        send("bm%d" % dy, SB.at[r, MID1:CUT], ram.at[dy], XM)

    def d_send(dx):
        send("d%d" % dx, SB.at[rel(dx, 1), CUT:ROWS], rd.at[dx], Y)

    def c_plain(dx, dy):
        if dx == 1:
            send("cp%db" % dy, SB.at[rel(1, dy), MID1:CUT], rbp.at[dy, MID1:CUT], XP)
        else:
            send("cm%db" % dy, SB.at[rel(3, dy), 0:MID1], rbm.at[dy, 0:MID1], XM)

    def c_added(dy):
        arrived("bp%d" % dy, "bm%d" % dy)

        def body(at):
            s, t = at(0), at(MID1)
            SB[rel(1, dy), s] = (T[rel(1, dy), s] + rap[dy, s].astype(f32)).astype(bf16)
            SB[rel(3, dy), t] = (T[rel(3, dy), t] + ram[dy, s].astype(f32)).astype(bf16)

        rows_loop(MID1, body)
        send("cp%da" % dy, SB.at[rel(1, dy), 0:MID1], rbp.at[dy, 0:MID1], XP)
        send("cm%da" % dy, SB.at[rel(3, dy), MID1:CUT], rbm.at[dy, MID1:CUT], XM)

    def e_send():
        arrived("cp1a", "cp1b", "cm1a", "cm1b")

        def body(at):
            s = at(0)
            total = T[rel(0, 1), s] + rbp[1, s].astype(f32) + rbm[1, s].astype(f32)
            SB[rel(0, 1), s] = total.astype(bf16)

        rows_loop(CUT, body)
        send("e", SB.at[rel(0, 1), 0:CUT], re, Y)

    def g_send():
        arrived("d2")

        def body(at):
            s, t = at(0), at(CUT)
            SB[rel(2, 0), t] = (T[rel(2, 0), t] + rd[2, s].astype(f32)).astype(bf16)

        rows_loop(ROWS - CUT, body)
        send("gp", SB.at[rel(2, 0), CUT:MID2], rgp, XP)
        send("gm", SB.at[rel(2, 0), MID2:ROWS], rgm, XM)

    def h_send():
        arrived("d1", "d3", "gp", "gm")
        half = MID2 - CUT

        def body(at):
            s, u, t, v = at(0), at(half), at(CUT), at(MID2)
            SB[rel(1, 0), t] = (T[rel(1, 0), t] + rd[1, s].astype(f32) + rgp[s].astype(f32)).astype(bf16)
            SB[rel(1, 0), v] = (T[rel(1, 0), v] + rd[1, u].astype(f32)).astype(bf16)
            SB[rel(3, 0), t] = (T[rel(3, 0), t] + rd[3, s].astype(f32)).astype(bf16)
            SB[rel(3, 0), v] = (T[rel(3, 0), v] + rd[3, u].astype(f32) + rgm[s].astype(f32)).astype(bf16)

        rows_loop(half, body)
        send("hpa", SB.at[rel(1, 0), CUT:MID2], rhp.at[0:half], XP)
        send("hma", SB.at[rel(3, 0), CUT:MID2], rhm.at[0:half], XM)
        send("hpb", SB.at[rel(1, 0), MID2:ROWS], rhp.at[half : ROWS - CUT], XP)
        send("hmb", SB.at[rel(3, 0), MID2:ROWS], rhm.at[half : ROWS - CUT], XM)

    def finish_high(part):
        arrived("d0", "hp" + part, "hm" + part)
        half = MID2 - CUT
        first = 0 if part == "a" else half

        def body(at):
            s, t = at(first), at(CUT + first)
            G[t] = T[rel(0, 0), t] + rd[0, s].astype(f32) + rhp[s].astype(f32) + rhm[s].astype(f32)

        rows_loop(half, body)

    def finish_low():
        arrived("cp0a", "cp0b", "cm0a", "cm0b")

        def body(at):
            s = at(0)
            G[s] = T[rel(0, 0), s] + rbp[0, s].astype(f32) + rbm[0, s].astype(f32)

        rows_loop(CUT, body)
        arrived("e")

        def body2(at):
            s = at(0)
            G[s] = G[s] + re[s].astype(f32)

        rows_loop(CUT, body2)

    def kv_half(slot, h):
        kv_wait()
        dst = KVs if slot == 1 else KVo

        @pl.loop(0, 2)
        def _(j):
            cols = pl.ds(pl.multiple_of(h * 512 + j * 256, 256), 256)
            weights = Wb[:, :, cols].reshape(HALF, 256)
            dst[:, cols] = jnp.dot(Xb[slot], weights, preferred_element_type=f32)

        if slot == 1:
            cols = slice(h * 512, h * 512 + 512)
            send("kv%d" % h, KVs.at[:, cols], KVr.at[:, cols], SIB)

    def kv_wait():
        if "w" not in here:
            here.add("w")
            load_w.wait()
        arrived("yP2_0", "yP2_1", "yP2_3", "yP2_2a", "yP2_2b", "xpfP1", "xmfP1", "xpfQ1", "xmfQ1")

    def kv_finish():
        arrived("kv0", "kv1")

        def body(at):
            s = at(0)
            KVb[s] = (KVo[s] + KVr[s]).astype(bf16)

        rows_loop(TOK, body)

    done = set()

    def all_sent(*later):
        for name, cp in sent.items():
            if name not in done and not name.startswith(later or ("none",)):
                done.add(name)
                cp.wait_send()

    z_start()
    own_term(4)
    own_term(7)
    both_terms(6)
    ring("L3", "L4", ((3, 0), (5, 1)))
    own_term(5)
    a_p2()
    ring("S2", "S3", ((2, 1), (6, 0)))
    both_terms(2)
    both_terms(5)
    b_send(1)
    both_terms(7)
    ring("L2", "L3", ((2, 0), (6, 1)))
    a_q1()
    own_term(1)
    ring("S1", "S2", ((1, 1), (7, 0)))
    ring("L1", "L2", ((1, 0), (7, 1)))
    c_plain(1, 1)
    c_plain(3, 1)
    a_p1()
    b_send(0)
    d_send(2)
    z_total()
    own_term(0)
    c_added(1)
    both_terms(1)
    a_fq1()
    d_send(1)
    both_terms(4)
    outer_step()
    own_term(3)
    a_p2far()
    g_send()
    share("q", 1)
    d_send(3)
    share("o", 2)
    both_terms(3)
    e_send()
    share("q", 2)
    both_terms(0)
    c_added(0)
    c_plain(1, 0)
    c_plain(3, 0)
    share("o", 3)
    kv_half(0, 0)
    kv_half(1, 0)
    d_send(0)
    h_send()
    share("q", 3)
    share("o", 4)
    kv_half(1, 1)
    share("q", 4)
    kv_half(0, 1)
    all_sent("c", "d0", "e", "h", "gpo4", "gmq4")
    finish_low()
    kv_finish()
    finish_high("a")
    finish_high("b")
    arrived("gpo4", "gmq4")

    all_sent()


def write_out(kv, grad, params, moment, weights, kv_out, grad_out, np_out, nm_out, lw_out, sem):
    z = lax.rem(lax.axis_index("replica"), 8)
    pairs = [(kv, kv_out), (grad, grad_out.at[0]), (params, np_out), (moment, nm_out)]
    for dz in range(8):
        for b in range(2):
            cols = pl.ds(pl.multiple_of(b * HALF + lax.rem(z + dz, 8) * FC, FC), FC)
            pairs.append((weights.at[dz, b], lw_out.at[:, cols]))
    copies = [pltpu.make_async_copy(src, dst, sem.at[i]) for i, (src, dst) in enumerate(pairs)]
    for cp in copies:
        cp.start()
    for cp in copies:
        cp.wait()


def on_device(inputs, projection, cotangent, pseudo_grad, outer_params, outer_momentum):
    any_ = pl.BlockSpec(memory_space=pl.ANY)
    inside = pl.BlockSpec(memory_space=pltpu.VMEM)
    vm = pltpu.VMEM
    scratch = [
        vm((2, TOK, HALF), bf16),
        vm((2, TOK, KV), bf16),
        vm((8, ROWS, KV), bf16),
        vm((8, ROWS, KV), bf16),
        vm((8, ROWS, KV), f32),
        vm((8, ROWS, KV), bf16),
        vm((TOK, KV), f32),
        vm((TOK, KV), f32),
        vm((TOK, KV), f32),
        vm((2, MID1, KV), bf16),
        vm((2, MID1, KV), bf16),
        vm((4, ROWS - CUT, KV), bf16),
        vm((2, CUT, KV), bf16),
        vm((2, CUT, KV), bf16),
        vm((CUT, KV), bf16),
        vm((MID2 - CUT, KV), bf16),
        vm((MID2 - CUT, KV), bf16),
        vm((ROWS - CUT, KV), bf16),
        vm((ROWS - CUT, KV), bf16),
        vm((8, 2, FR, FC), bf16),
        vm((2, 2, FR, FC), bf16),
        vm((5, 2, FR, FC), f32),
        vm((5, 2, FR, FC), f32),
        vm((2, FR, FC), f32),
        vm((FR, FC), f32),
        vm((FR, FC), f32),
        vm((FR, FC), f32),
        pltpu.SemaphoreType.DMA((len(MESSAGES),)),
        pltpu.SemaphoreType.DMA((len(MESSAGES),)),
        pltpu.SemaphoreType.DMA((32,)),
        pltpu.SemaphoreType.REGULAR((7,)),
    ]
    operands = (inputs, projection, cotangent, pseudo_grad, outer_params, outer_momentum)
    operands = [pltpu.with_memory_space_constraint(a, pltpu.HBM) for a in operands]
    results = pl.pallas_call(
        kernel,
        out_shape=(
            vm((TOK, KV), bf16),
            vm((ROWS, KV), f32),
            vm((FR, FC), f32),
            vm((FR, FC), f32),
            vm((8, 2, FR, FC), bf16),
        ),
        in_specs=[any_] * 6,
        out_specs=(inside,) * 5,
        scratch_shapes=scratch,
        compiler_params=pltpu.CompilerParams(
            collective_id=0, has_side_effects=True, vmem_limit_bytes=44 * 2**20
        ),
        cost_estimate=pl.CostEstimate(flops=6 * 10**9, bytes_accessed=3 * 10**7, transcendentals=0),
    )(*operands)
    results = [pltpu.with_memory_space_constraint(a, pltpu.VMEM) for a in results]
    return pl.pallas_call(
        write_out,
        out_shape=(
            jax.ShapeDtypeStruct((TOK, KV), bf16),
            jax.ShapeDtypeStruct((1, ROWS, KV), f32),
            jax.ShapeDtypeStruct((FR, FC), f32),
            jax.ShapeDtypeStruct((FR, FC), f32),
            jax.ShapeDtypeStruct((FR, D), bf16),
        ),
        in_specs=[inside] * 5,
        out_specs=(any_,) * 5,
        scratch_shapes=[pltpu.SemaphoreType.DMA((20,))],
        compiler_params=pltpu.CompilerParams(vmem_limit_bytes=44 * 2**20),
    )(*results)


def solution(mesh):
    return jax.shard_map(
        on_device,
        mesh=mesh,
        in_specs=(
            P(("replica", "fsdp"), None),
            P("replica", "fsdp", None),
            P(("replica", "fsdp"), None),
            P("replica", "fsdp", None),
            P("fsdp", "replica"),
            P("fsdp", "replica"),
        ),
        out_specs=(
            P(("replica", "fsdp"), None),
            P("replica", "fsdp", None),
            P("fsdp", "replica"),
            P("fsdp", "replica"),
            P("fsdp", None),
        ),
        check_vma=False,
    )
```
